32 devices in a mesh: tm: 4 (over y, core), space: 8 (over z, x).
Axes of the slice: x: 2, y: 2, z: 4, core: 2. Of those that a mesh axis runs over, the one named last changes fastest.
Arguments:
- sources: bfloat16 [4, 2, 4, 3, 12, 8, 128], P('tm', None, None, None, None, 'space'), may hold values from -6 to 6
- gauge_links: bfloat16 [4, 4, 2, 3, 3, 8, 128], P(None, 'tm', None, None, None, 'space'), may hold values from -2.5 to 2.5
- eigenvectors: bfloat16 [4, 128, 2, 3, 8, 128], P('tm', None, None, None, 'space'), may hold values from -0.109375 to 0.109375
- elementals: float32 [4, 2, 128, 128], P('tm', None, 'space'), may hold values from -0.375 to 0.375
Outputs:
- projected: float32 [4, 2, 4, 12, 128], P('tm', None, None, None, 'space')
- contracted: float32 [4, 2, 4, 12, 128], P('tm', None, None, None, 'space')
The draws below stay inside these ranges and needn't reach their ends.
All inputs are finite; a program needn't handle non-finite values.
Results may differ from the reference program's by a relative error of at most 0.0075.
Values may be sent and summed in bfloat16 or wider, within the bound.
A program may use at most 64 MiB of HBM per device.

```python
import jax
import jax.numpy as jnp
from jax import lax

NSRC = 12
NMODE = 128
LX = 8
LY = 16
NT = 4
NZ = 8


def raised(values, stream_key, source, target, shards_of, factor):
    def block_of(axis_at):
        return (jnp.arange(values.shape[axis_at]) // (values.shape[axis_at] // shards_of)).reshape((-1,) + (1,) * (values.ndim - 1 - axis_at))

    one_side = jax.random.permutation(stream_key, shards_of)[block_of(target)]
    other_side = (block_of(target) + shards_of // 2) % shards_of
    return jnp.where((block_of(source) == one_side) | (block_of(source) == other_side), factor * values, values)


def levels(rng, extent, shards, low, largest):
    def one(dim, parts):
        draws = jax.random.uniform(jax.random.fold_in(jax.random.fold_in(rng, 6), dim), (parts,), jnp.float32, low / len(shards), largest / len(shards))
        return jnp.repeat(jnp.exp(draws), extent[dim] // parts).reshape((-1,) + (1,) * (len(extent) - dim - 1))

    factor_of = one(*shards[0])
    for cut in shards[1:]:
        factor_of = factor_of * one(*cut)
    return factor_of


def centred(stream_key, extent, width, bound, split=(), kind=jnp.bfloat16):
    result = width * jax.random.normal(stream_key, extent, jnp.float32)
    if split:
        result = result * levels(stream_key, extent, split, -0.22, 0.18)
    return jnp.clip(result, -bound, bound).astype(kind)


def bell_draw_with(stream_key, shape, spread, bound, pieces, heavy, kind=jnp.bfloat16):
    entries = spread * jax.random.normal(stream_key, shape, jnp.float32)
    if pieces:
        entries = entries * levels(stream_key, shape, pieces, -0.22, 0.18)
    return jnp.clip(raised(entries, jax.random.fold_in(stream_key, 3), *heavy), -bound, bound).astype(kind)


def setup_inputs(seed: int = 0) -> dict:
    streams_of = jax.random.split(jax.random.key(seed), 5)
    return {
        "sources": centred(streams_of[0], (NT, 2, 4, 3, NSRC, NZ, LX * LY), 1.0, 6.0, ((0, 4), (5, 8))),
        "gauge_links": centred(streams_of[1], (4, NT, 2, 3, 3, NZ, LX * LY), 0.41, 2.5, ((1, 4), (5, 8))),
        "eigenvectors": bell_draw_with(streams_of[2], (NT, NMODE, 2, 3, NZ, LX * LY), (6 * LX * LY * NZ) ** -0.5, 0.109375, ((0, 4), (4, 8)), (4, 1, 8, 2.0)),
        "elementals": centred(streams_of[3], (NT, 2, NMODE, NMODE), (2 * NMODE) ** -0.5, 0.375, ((0, 4), (2, 8)), jnp.float32),
    }


highest = lax.Precision.HIGHEST
hopping = 0.125


def times_unit(value, sign):
    return (-sign * value[1], sign * value[0])


def mult_block(direction, first, second):
    if direction == 0:
        return times_unit(second, -1.0), times_unit(first, -1.0)
    if direction == 1:
        return (-second[0], -second[1]), first
    if direction == 2:
        return times_unit(first, -1.0), times_unit(second, 1.0)
    return first, second


def half_spinor(direction, pair, sign):
    upper_a = (pair[0][:, 0], pair[1][:, 0])
    upper_b = (pair[0][:, 1], pair[1][:, 1])
    lower_a = (pair[0][:, 2], pair[1][:, 2])
    lower_b = (pair[0][:, 3], pair[1][:, 3])
    moved_a, moved_b = mult_block(direction, lower_a, lower_b)
    real_part = jnp.stack([upper_a[0] + sign * moved_a[0], upper_b[0] + sign * moved_b[0]], 1)
    imag_part = jnp.stack([upper_a[1] + sign * moved_a[1], upper_b[1] + sign * moved_b[1]], 1)
    return real_part, imag_part


def rebuild(direction, pair, sign):
    first = (pair[0][:, 0], pair[1][:, 0])
    second = (pair[0][:, 1], pair[1][:, 1])
    if direction == 3:
        lower_a = (sign * first[0], sign * first[1])
        lower_b = (sign * second[0], sign * second[1])
    else:
        moved_a, moved_b = mult_block(direction, first, second)
        lower_a = (-sign * moved_a[0], -sign * moved_a[1])
        lower_b = (-sign * moved_b[0], -sign * moved_b[1])
    real_part = jnp.stack([first[0], second[0], lower_a[0], lower_b[0]], 1)
    imag_part = jnp.stack([first[1], second[1], lower_a[1], lower_b[1]], 1)
    return real_part, imag_part


def color_apply(link_re, link_im, field_re, field_im, dagger):
    out_re = []
    out_im = []
    for row in range(3):
        acc_re = 0.0
        acc_im = 0.0
        for col in range(3):
            if dagger:
                entry_re = link_re[:, col, row][:, None, None]
                entry_im = -link_im[:, col, row][:, None, None]
            else:
                entry_re = link_re[:, row, col][:, None, None]
                entry_im = link_im[:, row, col][:, None, None]
            vec_re = field_re[:, :, col]
            vec_im = field_im[:, :, col]
            acc_re = acc_re + entry_re * vec_re - entry_im * vec_im
            acc_im = acc_im + entry_re * vec_im + entry_im * vec_re
        out_re.append(acc_re)
        out_im.append(acc_im)
    return jnp.stack(out_re, 2), jnp.stack(out_im, 2)


def plane_shift(values, direction, stride, row_len):
    if direction == 1:
        return jnp.roll(values, -stride * row_len, axis=-1)
    column = jnp.arange(values.shape[-1]) % row_len
    if stride == 1:
        return jnp.where(column == row_len - 1, jnp.roll(values, row_len - 1, -1), jnp.roll(values, -1, -1))
    return jnp.where(column == 0, jnp.roll(values, -(row_len - 1), -1), jnp.roll(values, 1, -1))


def split_parts(values):
    widened = values.astype(jnp.float32)
    return widened[:, 0], widened[:, 1]


def stored(pair):
    return jnp.stack([pair[0], pair[1]], 1).astype(jnp.bfloat16)


def minus_chi(direction, pair):
    return stored(half_spinor(direction, pair, -1.0))


def plus_chi(direction, pair, link_pair):
    half = half_spinor(direction, pair, 1.0)
    return stored(color_apply(link_pair[0], link_pair[1], half[0], half[1], True))


def direction_term(direction, ahead, behind, link_pair):
    ahead_pair = split_parts(ahead)
    behind_pair = split_parts(behind)
    moved = color_apply(link_pair[0], link_pair[1], ahead_pair[0], ahead_pair[1], False)
    forward = rebuild(direction, moved, -1.0)
    backward = rebuild(direction, behind_pair, 1.0)
    return forward[0] + backward[0], forward[1] + backward[1]


def contract(matrices, values):
    def product(left, right):
        return jnp.einsum('tkl,tasl->task', left, right, precision=highest)
    real_part = product(matrices[:, 0], values[:, 0]) - product(matrices[:, 1], values[:, 1])
    imag_part = product(matrices[:, 0], values[:, 1]) + product(matrices[:, 1], values[:, 0])
    return jnp.stack([real_part, imag_part], 1)


def reference(sources, gauge_links, eigenvectors, elementals):
    link_here = [split_parts(gauge_links[direction]) for direction in range(4)]

    def polynomial(source_one):
        current = source_one
        base = source_one.astype(jnp.float32)
        slices = source_one.shape[0]
        tpos = jnp.arange(slices).reshape(-1, 1, 1, 1, 1, 1, 1)
        ahead_sign = jnp.where(tpos == slices - 1, -1.0, 1.0)
        behind_sign = jnp.where(tpos == 0, -1.0, 1.0)
        for sweep in range(3):
            pair = split_parts(current)
            result_re = 0.0
            result_im = 0.0
            for direction in range(4):
                minus = minus_chi(direction, pair)
                plus = plus_chi(direction, pair, link_here[direction])
                if direction < 2:
                    ahead = plane_shift(minus, direction, 1, LX)
                    behind = plane_shift(plus, direction, -1, LX)
                elif direction == 2:
                    ahead = jnp.roll(minus, -1, 5)
                    behind = jnp.roll(plus, 1, 5)
                else:
                    ahead = ahead_sign * jnp.roll(minus, -1, 0).astype(jnp.float32)
                    behind = behind_sign * jnp.roll(plus, 1, 0).astype(jnp.float32)
                term_re, term_im = direction_term(direction, ahead, behind, link_here[direction])
                result_re = result_re + term_re
                result_im = result_im + term_im
            current = (base + hopping * jnp.stack([result_re, result_im], 1)).astype(jnp.bfloat16)
        return current[:, :, :, :, 0]

    per_source = jnp.moveaxis(sources, 4, 0)[:, :, :, :, :, None]
    finals = jnp.moveaxis(lax.map(polynomial, per_source), 0, 4)

    def project_slice(pair):
        vectors, values = pair
        widened = vectors.astype(jnp.float32)
        spinor = values.astype(jnp.float32)
        stacked = jnp.stack([spinor, jnp.stack([spinor[1], -spinor[0]])])
        return jnp.einsum('krczp,oracszp->oask', widened, stacked, precision=highest)

    projected = lax.map(project_slice, (eigenvectors, finals))
    contracted = contract(elementals, projected)
    return projected, contracted
```

```python
import functools

import jax
import jax.numpy as jnp
from jax import lax
from jax.experimental import pallas as pl
from jax.experimental.pallas import tpu as pltpu
from jax.sharding import PartitionSpec as P

LX = 8
HOPPING = 0.125
SWEEPS = 3
MESH = pl.DeviceIdType.MESH
f32 = jnp.float32
bf16 = jnp.bfloat16


def each(lower, upper, body):
    if upper - lower <= 16:
        for index in range(lower, upper):
            body(index)
    else:
        lax.fori_loop(lower, upper, lambda index, carry: (body(index), carry)[1], 0)


def kernel(
    slices, peers, nsrc, modes_dev,
    src_hbm, link_hbm, vec_hbm, elem_hbm,
    proj_ref, cont_ref,
    src_in, link_in, vec_in, elem_in, load_sem,
    wide, link_wide, links, base, field, swap, vec_wide,
    halo_out, halo_in, halo_send, halo_recv,
    elem_all, elem_full, elem_send, elem_recv,
    left_mat, right_mat, sums, part_out, part_in, part_send, part_recv, turned,
):
    rows = 2 * nsrc
    tiles = rows // 8
    lanes = base.shape[-1]
    nmode = peers * modes_dev
    t = lax.axis_index("tm")
    me = lax.axis_index("space")
    t_up, t_down = lax.rem(t + 1, slices), lax.rem(t + slices - 1, slices)
    z_up, z_down = lax.rem(me + 1, peers), lax.rem(me + peers - 1, peers)

    barrier = pltpu.get_barrier_semaphore()

    def greet(off):
        pl.semaphore_signal(
            barrier, inc=1, device_id=(t, lax.rem(me + off, peers)), device_id_type=MESH
        )

    for near in (t_up, t_down):
        pl.semaphore_signal(barrier, inc=1, device_id=(near, me), device_id_type=MESH)
    each(1, peers, greet)

    loads = [
        pltpu.make_async_copy(a, b, load_sem.at[i])
        for i, (a, b) in enumerate(
            ((src_hbm, src_in), (link_hbm, link_in), (elem_hbm, elem_in), (vec_hbm, vec_in))
        )
    ]
    for load in loads:
        load.start()

    loads[1].wait()
    link_wide[...] = link_in[...].astype(f32)
    for mu in range(4):
        for i in range(3):
            for j in range(3):
                for part in range(2):
                    row = ((mu * 3 + i) * 3 + j) * 2 + part
                    links[mu, part, i, j] = jnp.broadcast_to(
                        link_wide[row : row + 1, :], (8, lanes)
                    )
    loads[0].wait()
    wide[...] = src_in[...].astype(f32)
    for pc in range(6):
        for spin in range(4):
            piece = wide[pl.ds(pc * 4 * nsrc + spin, nsrc, stride=4), :]
            base[pc, spin * nsrc : (spin + 1) * nsrc, :] = piece
            field[pc, spin * nsrc : (spin + 1) * nsrc, :] = piece
            if spin == 2:
                field[pc, 4 * nsrc : 5 * nsrc, :] = piece

    row_at = lax.broadcasted_iota(jnp.int32, (tiles, 8, lanes), 0) * 8
    row_at = row_at + lax.broadcasted_iota(jnp.int32, (tiles, 8, lanes), 1)
    spin_sign = jnp.where(row_at < nsrc, 1.0, -1.0).astype(f32)[None]
    column = lax.broadcasted_iota(jnp.int32, (1, 1, 8, lanes), 3) % LX
    ahead_sign = jnp.where(t == slices - 1, -1.0, 1.0).astype(f32)
    behind_sign = jnp.where(t == 0, -1.0, 1.0).astype(f32)

    def tiled(value):
        return value.reshape(3, tiles, 8, lanes)

    def apply(mu, pair, dagger):
        re, im = pair
        out_re = out_im = None
        for j in range(3):
            if dagger:
                g_re, g_im = links[mu, 0, j], links[mu, 1, j]
            else:
                g_re, g_im = links[mu, 0, :, j], links[mu, 1, :, j]
            g_re, g_im = g_re[:, None], g_im[:, None]
            v_re, v_im = re[j][None], im[j][None]
            if dagger:
                add_re, add_im = g_re * v_re + g_im * v_im, g_re * v_im - g_im * v_re
            else:
                add_re, add_im = g_re * v_re - g_im * v_im, g_re * v_im + g_im * v_re
            out_re = add_re if out_re is None else out_re + add_re
            out_im = add_im if out_im is None else out_im + add_im
        return out_re, out_im

    def shift(pair, direction, ahead):
        out = []
        for v in pair:
            flat = v.reshape(3 * rows, lanes)
            if direction == 1:
                got = pltpu.roll(flat, lanes - LX if ahead else LX, 1)
                out.append(tiled(got))
            else:
                near = tiled(pltpu.roll(flat, lanes - 1 if ahead else 1, 1))
                wrap = tiled(pltpu.roll(flat, LX - 1 if ahead else lanes - LX + 1, 1))
                out.append(jnp.where(column == (LX - 1 if ahead else 0), wrap, near))
        return tuple(out)

    def packed(pair):
        return jnp.concatenate([v.reshape(3 * rows, lanes) for v in pair], 0).astype(bf16)

    def unpacked(value):
        value = value.astype(f32)
        return tiled(value[: 3 * rows]), tiled(value[3 * rows :])

    def halo(sweep, way):
        target = ((t_down, me), (t_up, me), (t, z_down), (t, z_up))[way]
        return pltpu.make_async_remote_copy(
            src_ref=halo_out.at[sweep, way],
            dst_ref=halo_in.at[sweep, way],
            send_sem=halo_send.at[sweep, way],
            recv_sem=halo_recv.at[sweep, way],
            device_id=target,
            device_id_type=MESH,
        )

    def elem_copy(to, slot):
        return pltpu.make_async_remote_copy(
            src_ref=elem_all.at[me],
            dst_ref=elem_all.at[slot],
            send_sem=elem_send.at[to],
            recv_sem=elem_recv.at[slot],
            device_id=(t, to),
            device_id_type=MESH,
        )

    def part_copy(to, slot):
        return pltpu.make_async_remote_copy(
            src_ref=part_out.at[to],
            dst_ref=part_in.at[slot],
            send_sem=part_send.at[to],
            recv_sem=part_recv.at[slot],
            device_id=(t, to),
            device_id_type=MESH,
        )

    for sweep in range(SWEEPS):
        up = [tiled(field[3 * i : 3 * i + 3, 0:rows, :]) for i in range(2)]
        low = [tiled(field[3 * i : 3 * i + 3, rows : 2 * rows, :]) for i in range(2)]
        turn = (spin_sign * low[1], -(spin_sign * low[0]))
        sent = [halo(sweep, way) for way in range(4)]
        halo_out[sweep, 2] = packed((up[0] - turn[0], up[1] - turn[1]))
        if sweep == 0:
            pl.semaphore_wait(barrier, peers + 1)
        sent[2].start()
        halo_out[sweep, 3] = packed(apply(2, (up[0] + turn[0], up[1] + turn[1]), True))
        sent[3].start()
        halo_out[sweep, 0] = packed((up[0] - low[0], up[1] - low[1]))
        sent[0].start()
        halo_out[sweep, 1] = packed(apply(3, (up[0] + low[0], up[1] + low[1]), True))
        sent[1].start()

        if sweep == 0:
            loads[2].wait()
            elem_all[me] = elem_in[...].astype(elem_all.dtype)
            each(1, peers, lambda off: elem_copy(lax.rem(me + off, peers), me).start())

        swapped = [
            tiled(field[3 * i : 3 * i + 3, rows + nsrc : 2 * rows + nsrc, :]) for i in range(2)
        ]
        turned_x = (swapped[1], -swapped[0])
        turned_y = (-(spin_sign * swapped[0]), -(spin_sign * swapped[1]))
        ahead = {}
        behind = {}
        for mu, moved in ((0, turned_x), (1, turned_y)):
            ahead[mu] = apply(
                mu, shift((up[0] - moved[0], up[1] - moved[1]), mu, True), False
            )
            behind[mu] = shift(
                apply(mu, (up[0] + moved[0], up[1] + moved[1]), True), mu, False
            )
        upper = [ahead[0][i] + behind[0][i] + ahead[1][i] + behind[1][i] for i in range(2)]
        dx = [behind[0][i] - ahead[0][i] for i in range(2)]
        dy = [behind[1][i] - ahead[1][i] for i in range(2)]
        cross = (-dx[1] - spin_sign * dy[0], dx[0] - spin_sign * dy[1])
        for i in range(2):
            flat = cross[i].reshape(3, rows, lanes)
            swap[3 * i : 3 * i + 3, 0:rows, :] = flat
            swap[3 * i : 3 * i + 3, rows : rows + nsrc, :] = flat[:, :nsrc]
        lower = [tiled(swap[3 * i : 3 * i + 3, nsrc : nsrc + rows, :]) for i in range(2)]

        if sweep == 0:
            loads[3].wait()
            vec_wide[...] = vec_in[...].astype(f32)
            for j in range(6):
                left_mat[0:nmode, j * lanes : (j + 1) * lanes] = vec_wide[
                    pl.ds(j, nmode, stride=6), :
                ].astype(bf16)
        if sweep == 1:
            each(
                1, peers,
                lambda off: elem_copy(lax.rem(me + off, peers), lax.rem(me + off, peers)).wait_recv(),
            )
            for p in range(peers):
                for part in range(2):
                    elem_full[part, p * modes_dev : (p + 1) * modes_dev, :] = elem_all[
                        p, part
                    ].astype(f32)
            e_re, e_im = elem_full[0].astype(bf16), elem_full[1].astype(bf16)
            blocks = jnp.concatenate(
                [
                    jnp.concatenate([e_re, e_im], 1),
                    jnp.concatenate([-e_im, e_re], 1),
                ],
                0,
            )
            for c in range(3):
                both = jnp.concatenate(
                    [
                        left_mat[0:nmode, (2 * c + part) * lanes : (2 * c + part + 1) * lanes]
                        for part in range(2)
                    ],
                    0,
                )
                mixed = jnp.dot(blocks, both, preferred_element_type=f32).astype(bf16)
                for part in range(2):
                    left_mat[
                        nmode : 2 * nmode, (2 * c + part) * lanes : (2 * c + part + 1) * lanes
                    ] = mixed[part * nmode : (part + 1) * nmode]

        sent[0].wait_recv()
        f_t = apply(3, unpacked(halo_in[sweep, 0]), False)
        sent[1].wait_recv()
        b_t = unpacked(halo_in[sweep, 1])
        f_t = [ahead_sign * v for v in f_t]
        b_t = [behind_sign * v for v in b_t]
        upper = [upper[i] + f_t[i] + b_t[i] for i in range(2)]
        lower = [lower[i] + b_t[i] - f_t[i] for i in range(2)]
        sent[2].wait_recv()
        f_z = apply(2, unpacked(halo_in[sweep, 2]), False)
        sent[3].wait_recv()
        b_z = unpacked(halo_in[sweep, 3])
        dz = [b_z[i] - f_z[i] for i in range(2)]
        upper = [upper[i] + f_z[i] + b_z[i] for i in range(2)]
        lower = [lower[0] - spin_sign * dz[1], lower[1] + spin_sign * dz[0]]
        for i in range(2):
            at = slice(3 * i, 3 * i + 3)
            new_up = base[at, 0:rows, :] + HOPPING * upper[i].reshape(3, rows, lanes)
            new_low = base[at, rows : 2 * rows, :] + HOPPING * lower[i].reshape(3, rows, lanes)
            new_up = new_up.astype(bf16).astype(f32)
            new_low = new_low.astype(bf16).astype(f32)
            field[at, 0:rows, :] = new_up
            field[at, rows : 2 * rows, :] = new_low
            if sweep < SWEEPS - 1:
                field[at, 2 * rows : 2 * rows + nsrc, :] = new_low[:, :nsrc]

    for pc in range(6):
        for spin in range(4):
            wide[pl.ds(pc * 4 * nsrc + spin, nsrc, stride=4), :] = field[
                pc, spin * nsrc : (spin + 1) * nsrc, :
            ]
    count = 4 * nsrc
    for c in range(3):
        re = wide[c * count : (c + 1) * count, :]
        im = wide[(3 + c) * count : (4 + c) * count, :]
        at = 2 * c * lanes
        right_mat[:, at : at + lanes] = jnp.concatenate([re, im], 0).astype(bf16)
        right_mat[:, at + lanes : at + 2 * lanes] = jnp.concatenate([im, -re], 0).astype(bf16)
    sums[:, 0 : 2 * count] = lax.dot_general(
        left_mat[...], right_mat[...], (((1,), (1,)), ((), ())), preferred_element_type=f32
    )
    for p in range(peers):
        for o in range(2):
            at = o * nmode + p * modes_dev
            part_out[p, o] = sums[at : at + modes_dev, :].astype(part_out.dtype)
    each(1, peers, lambda off: part_copy(lax.rem(me + off, peers), me).start())

    turned[...] = jnp.zeros_like(turned)
    for o in range(2):
        turned[o * modes_dev : (o + 1) * modes_dev, :] = part_out[me, o].astype(f32)

    def gather(off):
        p = lax.rem(me + off, peers)
        part_copy(p, p).wait_recv()
        for o in range(2):
            turned[o * modes_dev : (o + 1) * modes_dev, :] += part_in[p, o].astype(f32)

    each(1, peers, gather)
    flipped = turned[...].T
    proj_ref[...] = flipped[0 : 2 * count, 0:modes_dev]
    cont_ref[...] = flipped[0 : 2 * count, modes_dev : 2 * modes_dev]

    for sweep in range(SWEEPS):
        for way in range(4):
            halo(sweep, way).wait_send()

    def settle(off):
        p = lax.rem(me + off, peers)
        elem_copy(p, me).wait_send()
        part_copy(p, me).wait_send()

    each(1, peers, settle)


def local(sources, gauge_links, eigenvectors, elementals):
    slices, peers = lax.axis_size("tm"), lax.axis_size("space")
    _, _, _, _, nsrc, _, lanes = sources.shape
    nmode = eigenvectors.shape[1]
    modes_dev = elementals.shape[2]
    src = sources.transpose(0, 1, 3, 4, 5, 2, 6).reshape(24 * nsrc, lanes)
    link = gauge_links.transpose(0, 1, 3, 4, 5, 2, 6).reshape(72, lanes)
    vec = eigenvectors.transpose(0, 1, 3, 4, 2, 5).reshape(6 * nmode, lanes)
    elem = elementals.reshape(2, modes_dev, nmode)
    rows = 2 * nsrc
    kind = bf16 if modes_dev % 16 == 0 else f32
    outs = jax.ShapeDtypeStruct((8 * nsrc, modes_dev), f32)
    dma = pltpu.SemaphoreType.DMA
    proj, cont = pl.pallas_call(
        functools.partial(kernel, slices, peers, nsrc, modes_dev),
        out_shape=(outs, outs),
        in_specs=[pl.BlockSpec(memory_space=pl.ANY)] * 4,
        out_specs=[pl.BlockSpec(memory_space=pltpu.VMEM)] * 2,
        scratch_shapes=[
            pltpu.VMEM(src.shape, bf16),
            pltpu.VMEM(link.shape, bf16),
            pltpu.VMEM(vec.shape, bf16),
            pltpu.VMEM(elem.shape, f32),
            dma((4,)),
            pltpu.VMEM(src.shape, f32),
            pltpu.VMEM(link.shape, f32),
            pltpu.VMEM((4, 2, 3, 3, 8, lanes), f32),
            pltpu.VMEM((6, 2 * rows, lanes), f32),
            pltpu.VMEM((6, 2 * rows + 16, lanes), f32),
            pltpu.VMEM((6, rows + 16, lanes), f32),
            pltpu.VMEM(vec.shape, f32),
            pltpu.VMEM((SWEEPS, 4, 6 * rows, lanes), bf16),
            pltpu.VMEM((SWEEPS, 4, 6 * rows, lanes), bf16),
            dma((SWEEPS, 4)),
            dma((SWEEPS, 4)),
            pltpu.VMEM((peers, 2, modes_dev, nmode), kind),
            pltpu.VMEM((2, nmode, nmode), f32),
            dma((peers,)),
            dma((peers,)),
            pltpu.VMEM((2 * nmode, 6 * lanes), bf16),
            pltpu.VMEM((8 * nsrc, 6 * lanes), bf16),
            pltpu.VMEM((2 * nmode, 128), f32),
            pltpu.VMEM((peers, 2, modes_dev, 128), kind),
            pltpu.VMEM((peers, 2, modes_dev, 128), kind),
            dma((peers,)),
            dma((peers,)),
            pltpu.VMEM((128, 128), f32),
        ],
        compiler_params=pltpu.CompilerParams(
            collective_id=0, has_side_effects=True, vmem_limit_bytes=32 * 1024 * 1024
        ),
        cost_estimate=pl.CostEstimate(
            flops=200_000_000, bytes_accessed=1_000_000, transcendentals=0
        ),
    )(src, link, vec, elem)

    def placed(out):
        return out.reshape(1, 2, nsrc, 4, modes_dev).transpose(0, 1, 3, 2, 4)

    return placed(proj), placed(cont)


def solution(mesh):
    placed = (
        P("tm", None, None, None, None, "space", None),
        P(None, "tm", None, None, None, "space", None),
        P("tm", None, None, None, "space", None),
        P("tm", None, "space", None),
    )
    return jax.shard_map(
        local,
        mesh=mesh,
        in_specs=placed,
        out_specs=(P("tm", None, None, None, "space"), P("tm", None, None, None, "space")),
        check_vma=False,
    )
```

```python
import functools

import jax
import jax.numpy as jnp
from jax import lax
from jax.experimental import pallas as pl
from jax.experimental.pallas import tpu as pltpu
from jax.sharding import PartitionSpec as P

LX = 8
HOPPING = 0.125
SWEEPS = 3
GROUP = 4
MESH = pl.DeviceIdType.MESH
f32 = jnp.float32
bf16 = jnp.bfloat16


def each(lower, upper, body):
    if upper - lower <= 16:
        for index in range(lower, upper):
            body(index)
    else:
        lax.fori_loop(lower, upper, lambda index, carry: (body(index), carry)[1], 0)


def kernel(
    slices, peers, nsrc, modes_dev,
    src_hbm, link_hbm, vec_hbm, elem_hbm,
    proj_ref, cont_ref,
    src_in, link_in, vec_in, elem_in, load_sem,
    wide, link_wide, links, base, field, hops, vec_wide,
    halo_out, halo_in, halo_send, halo_recv,
    elem_all, elem_full, elem_send, elem_recv,
    left_mat, right_mat, sums, part_out, part_in, part_send, part_recv, turned,
):
    groups = nsrc // GROUP
    half = 2 * GROUP
    lanes = base.shape[-1]
    nmode = peers * modes_dev
    t = lax.axis_index("tm")
    me = lax.axis_index("space")
    t_up, t_down = lax.rem(t + 1, slices), lax.rem(t + slices - 1, slices)
    z_up, z_down = lax.rem(me + 1, peers), lax.rem(me + peers - 1, peers)

    barrier = pltpu.get_barrier_semaphore()

    def greet(off):
        pl.semaphore_signal(
            barrier, inc=1, device_id=(t, lax.rem(me + off, peers)), device_id_type=MESH
        )

    for near in (t_up, t_down):
        pl.semaphore_signal(barrier, inc=1, device_id=(near, me), device_id_type=MESH)
    each(1, peers, greet)

    loads = [
        pltpu.make_async_copy(a, b, load_sem.at[i])
        for i, (a, b) in enumerate(
            ((src_hbm, src_in), (link_hbm, link_in), (elem_hbm, elem_in), (vec_hbm, vec_in))
        )
    ]
    for load in loads:
        load.start()

    row_at = lax.broadcasted_iota(jnp.int32, (1, half, lanes), 1)
    spin_sign = jnp.where(row_at < GROUP, 1.0, -1.0).astype(f32)
    column = lax.broadcasted_iota(jnp.int32, (1, half, lanes), 2) % LX
    ahead_sign = jnp.where(t == slices - 1, -1.0, 1.0).astype(f32)
    behind_sign = jnp.where(t == 0, -1.0, 1.0).astype(f32)

    def apply(mu, pair, dagger):
        re, im = pair
        out_re = out_im = None
        for j in range(3):
            if dagger:
                g_re, g_im = links[mu, 0, j], links[mu, 1, j]
            else:
                g_re, g_im = links[mu, 0, :, j], links[mu, 1, :, j]
            v_re, v_im = re[j][None], im[j][None]
            if dagger:
                add_re, add_im = g_re * v_re + g_im * v_im, g_re * v_im - g_im * v_re
            else:
                add_re, add_im = g_re * v_re - g_im * v_im, g_re * v_im + g_im * v_re
            out_re = add_re if out_re is None else out_re + add_re
            out_im = add_im if out_im is None else out_im + add_im
        return out_re, out_im

    def shift(pair, direction, ahead):
        out = []
        for v in pair:
            if direction == 1:
                out.append(pltpu.roll(v, lanes - LX if ahead else LX, 2))
            else:
                near = pltpu.roll(v, lanes - 1 if ahead else 1, 2)
                wrap = pltpu.roll(v, LX - 1 if ahead else lanes - LX + 1, 2)
                out.append(jnp.where(column == (LX - 1 if ahead else 0), wrap, near))
        return tuple(out)

    def packed(pair):
        return jnp.concatenate([v.reshape(3 * half, lanes) for v in pair], 0).astype(bf16)

    def unpacked(value):
        value = value.astype(f32).reshape(6, half, lanes)
        return value[:3], value[3:]

    def halo(sweep, g, way):
        at = (sweep * groups + g) * 4 + way
        target = ((t_down, me), (t_up, me), (t, z_down), (t, z_up))[way]
        return pltpu.make_async_remote_copy(
            src_ref=halo_out.at[at],
            dst_ref=halo_in.at[at],
            send_sem=halo_send.at[at],
            recv_sem=halo_recv.at[at],
            device_id=target,
            device_id_type=MESH,
        )

    def send(sweep, g, way, pair):
        halo_out[(sweep * groups + g) * 4 + way] = packed(pair)
        halo(sweep, g, way).start()

    def receive(sweep, g, way):
        halo(sweep, g, way).wait_recv()
        return unpacked(halo_in[(sweep * groups + g) * 4 + way])

    def elem_copy(to, slot):
        return pltpu.make_async_remote_copy(
            src_ref=elem_all.at[me],
            dst_ref=elem_all.at[slot],
            send_sem=elem_send.at[to],
            recv_sem=elem_recv.at[slot],
            device_id=(t, to),
            device_id_type=MESH,
        )

    def part_copy(to, slot):
        return pltpu.make_async_remote_copy(
            src_ref=part_out.at[to],
            dst_ref=part_in.at[slot],
            send_sem=part_send.at[to],
            recv_sem=part_recv.at[slot],
            device_id=(t, to),
            device_id_type=MESH,
        )

    def parts_of(g):
        up = [field[g, 3 * i : 3 * i + 3, 0:half, :] for i in range(2)]
        low = [field[g, 3 * i : 3 * i + 3, half : 2 * half, :] for i in range(2)]
        return up, low

    def turn_z(low):
        return spin_sign * low[1], -(spin_sign * low[0])

    def send_minus(sweep, g):
        up, low = parts_of(g)
        turn = turn_z(low)
        send(sweep, g, 2, (up[0] - turn[0], up[1] - turn[1]))
        send(sweep, g, 0, (up[0] - low[0], up[1] - low[1]))

    def send_plus(sweep, g):
        up, low = parts_of(g)
        turn = turn_z(low)
        send(sweep, g, 3, apply(2, (up[0] + turn[0], up[1] + turn[1]), True))
        send(sweep, g, 1, apply(3, (up[0] + low[0], up[1] + low[1]), True))

    def plane(g):
        up, low = parts_of(g)
        swapped = [pltpu.roll(v, GROUP, 1) for v in low]
        turned_x = (swapped[1], -swapped[0])
        turned_y = (-(spin_sign * swapped[0]), -(spin_sign * swapped[1]))
        ahead = {}
        behind = {}
        for mu, moved in ((0, turned_x), (1, turned_y)):
            ahead[mu] = apply(
                mu, shift((up[0] - moved[0], up[1] - moved[1]), mu, True), False
            )
            behind[mu] = shift(
                apply(mu, (up[0] + moved[0], up[1] + moved[1]), True), mu, False
            )
        dx = [behind[0][i] - ahead[0][i] for i in range(2)]
        dy = [behind[1][i] - ahead[1][i] for i in range(2)]
        cross = (-dx[1] - spin_sign * dy[0], dx[0] - spin_sign * dy[1])
        for i in range(2):
            hops[g, i] = ahead[0][i] + behind[0][i] + ahead[1][i] + behind[1][i]
            hops[g, 2 + i] = pltpu.roll(cross[i], GROUP, 1)

    def finish(sweep, g):
        f_t = apply(3, receive(sweep, g, 0), False)
        b_t = receive(sweep, g, 1)
        f_t = [ahead_sign * v for v in f_t]
        b_t = [behind_sign * v for v in b_t]
        f_z = apply(2, receive(sweep, g, 2), False)
        b_z = receive(sweep, g, 3)
        dz = [b_z[i] - f_z[i] for i in range(2)]
        upper = [hops[g, i] + f_t[i] + b_t[i] + f_z[i] + b_z[i] for i in range(2)]
        lower = [hops[g, 2 + i] + b_t[i] - f_t[i] for i in range(2)]
        lower = [lower[0] - spin_sign * dz[1], lower[1] + spin_sign * dz[0]]
        for i in range(2):
            at = slice(3 * i, 3 * i + 3)
            new_up = base[g, at, 0:half, :] + HOPPING * upper[i]
            new_low = base[g, at, half : 2 * half, :] + HOPPING * lower[i]
            field[g, at, 0:half, :] = new_up.astype(bf16).astype(f32)
            field[g, at, half : 2 * half, :] = new_low.astype(bf16).astype(f32)

    loads[0].wait()
    wide[...] = src_in[...].astype(f32)
    for g in range(groups):
        for pc in range(6):
            for spin in range(4):
                piece = wide[pl.ds((pc * nsrc + g * GROUP) * 4 + spin, GROUP, stride=4), :]
                base[g, pc, spin * GROUP : (spin + 1) * GROUP, :] = piece
                field[g, pc, spin * GROUP : (spin + 1) * GROUP, :] = piece
    pl.semaphore_wait(barrier, peers + 1)
    for g in range(groups):
        send_minus(0, g)

    loads[1].wait()
    link_wide[...] = link_in[...].astype(f32)
    for mu in (2, 3, 0, 1):
        for i in range(3):
            for j in range(3):
                for part in range(2):
                    row = ((mu * 3 + i) * 3 + j) * 2 + part
                    links[mu, part, i, j] = jnp.broadcast_to(
                        link_wide[row : row + 1, :], (half, lanes)
                    )
    for g in range(groups):
        send_plus(0, g)

    loads[2].wait()
    elem_all[me] = elem_in[...].astype(elem_all.dtype)
    each(1, peers, lambda off: elem_copy(lax.rem(me + off, peers), me).start())
    for g in range(groups):
        plane(g)

    loads[3].wait()
    vec_wide[...] = vec_in[...].astype(f32)
    for j in range(6):
        left_mat[0:nmode, j * lanes : (j + 1) * lanes] = vec_wide[
            pl.ds(j, nmode, stride=6), :
        ].astype(bf16)

    for sweep in range(1, SWEEPS):
        for g in range(groups):
            finish(sweep - 1, g)
            send_minus(sweep, g)
            send_plus(sweep, g)
        for g in range(groups):
            plane(g)
        if sweep == 1:
            def arrive(off):
                p = lax.rem(me + off, peers)
                elem_copy(p, p).wait_recv()

            each(1, peers, arrive)
            for p in range(peers):
                for part in range(2):
                    elem_full[part, p * modes_dev : (p + 1) * modes_dev, :] = elem_all[
                        p, part
                    ].astype(f32)
            e_re, e_im = elem_full[0].astype(bf16), elem_full[1].astype(bf16)
            blocks = jnp.concatenate(
                [
                    jnp.concatenate([e_re, e_im], 1),
                    jnp.concatenate([-e_im, e_re], 1),
                ],
                0,
            )
            for c in range(3):
                both = jnp.concatenate(
                    [
                        left_mat[0:nmode, (2 * c + part) * lanes : (2 * c + part + 1) * lanes]
                        for part in range(2)
                    ],
                    0,
                )
                mixed = jnp.dot(blocks, both, preferred_element_type=f32).astype(bf16)
                for part in range(2):
                    left_mat[
                        nmode : 2 * nmode, (2 * c + part) * lanes : (2 * c + part + 1) * lanes
                    ] = mixed[part * nmode : (part + 1) * nmode]

    for g in range(groups):
        finish(SWEEPS - 1, g)
        for pc in range(6):
            for spin in range(4):
                wide[pl.ds((pc * nsrc + g * GROUP) * 4 + spin, GROUP, stride=4), :] = field[
                    g, pc, spin * GROUP : (spin + 1) * GROUP, :
                ]
    count = 4 * nsrc
    for c in range(3):
        re = wide[c * count : (c + 1) * count, :]
        im = wide[(3 + c) * count : (4 + c) * count, :]
        at = 2 * c * lanes
        right_mat[:, at : at + lanes] = jnp.concatenate([re, im], 0).astype(bf16)
        right_mat[:, at + lanes : at + 2 * lanes] = jnp.concatenate([im, -re], 0).astype(bf16)
    sums[:, 0 : 2 * count] = lax.dot_general(
        left_mat[...], right_mat[...], (((1,), (1,)), ((), ())), preferred_element_type=f32
    )
    for p in range(peers):
        for o in range(2):
            at = o * nmode + p * modes_dev
            part_out[p, o] = sums[at : at + modes_dev, :].astype(part_out.dtype)
    each(1, peers, lambda off: part_copy(lax.rem(me + off, peers), me).start())

    turned[...] = jnp.zeros_like(turned)
    for o in range(2):
        turned[o * modes_dev : (o + 1) * modes_dev, :] = part_out[me, o].astype(f32)

    def settle(off):
        p = lax.rem(me + off, peers)
        elem_copy(p, me).wait_send()
        part_copy(p, me).wait_send()

    for sweep in range(SWEEPS):
        for g in range(groups):
            for way in range(4):
                halo(sweep, g, way).wait_send()
    each(1, peers, settle)

    def gather(off):
        p = lax.rem(me + off, peers)
        part_copy(p, p).wait_recv()
        for o in range(2):
            turned[o * modes_dev : (o + 1) * modes_dev, :] += part_in[p, o].astype(f32)

    each(1, peers, gather)
    flipped = turned[...].T
    proj_ref[...] = flipped[0 : 2 * count, 0:modes_dev]
    cont_ref[...] = flipped[0 : 2 * count, modes_dev : 2 * modes_dev]


def local(sources, gauge_links, eigenvectors, elementals):
    slices, peers = lax.axis_size("tm"), lax.axis_size("space")
    _, _, _, _, nsrc, _, lanes = sources.shape
    nmode = eigenvectors.shape[1]
    modes_dev = elementals.shape[2]
    src = sources.transpose(0, 1, 3, 4, 5, 2, 6).reshape(24 * nsrc, lanes)
    link = gauge_links.transpose(0, 1, 3, 4, 5, 2, 6).reshape(72, lanes)
    vec = eigenvectors.transpose(0, 1, 3, 4, 2, 5).reshape(6 * nmode, lanes)
    elem = elementals.reshape(2, modes_dev, nmode)
    groups, half = nsrc // GROUP, 2 * GROUP
    halos = SWEEPS * groups * 4
    kind = bf16 if modes_dev % 16 == 0 else f32
    outs = jax.ShapeDtypeStruct((8 * nsrc, modes_dev), f32)
    dma = pltpu.SemaphoreType.DMA
    proj, cont = pl.pallas_call(
        functools.partial(kernel, slices, peers, nsrc, modes_dev),
        out_shape=(outs, outs),
        in_specs=[pl.BlockSpec(memory_space=pl.ANY)] * 4,
        out_specs=[pl.BlockSpec(memory_space=pltpu.VMEM)] * 2,
        scratch_shapes=[
            pltpu.VMEM(src.shape, bf16),
            pltpu.VMEM(link.shape, bf16),
            pltpu.VMEM(vec.shape, bf16),
            pltpu.VMEM(elem.shape, f32),
            dma((4,)),
            pltpu.VMEM(src.shape, f32),
            pltpu.VMEM(link.shape, f32),
            pltpu.VMEM((4, 2, 3, 3, half, lanes), f32),
            pltpu.VMEM((groups, 6, 2 * half, lanes), f32),
            pltpu.VMEM((groups, 6, 2 * half, lanes), f32),
            pltpu.VMEM((groups, 4, 3, half, lanes), f32),
            pltpu.VMEM(vec.shape, f32),
            pltpu.VMEM((halos, 6 * half, lanes), bf16),
            pltpu.VMEM((halos, 6 * half, lanes), bf16),
            dma((halos,)),
            dma((halos,)),
            pltpu.VMEM((peers, 2, modes_dev, nmode), kind),
            pltpu.VMEM((2, nmode, nmode), f32),
            dma((peers,)),
            dma((peers,)),
            pltpu.VMEM((2 * nmode, 6 * lanes), bf16),
            pltpu.VMEM((8 * nsrc, 6 * lanes), bf16),
            pltpu.VMEM((2 * nmode, 128), f32),
            pltpu.VMEM((peers, 2, modes_dev, 128), kind),
            pltpu.VMEM((peers, 2, modes_dev, 128), kind),
            dma((peers,)),
            dma((peers,)),
            pltpu.VMEM((128, 128), f32),
        ],
        compiler_params=pltpu.CompilerParams(
            collective_id=0, has_side_effects=True, vmem_limit_bytes=60 * 1024 * 1024
        ),
        cost_estimate=pl.CostEstimate(
            flops=200_000_000, bytes_accessed=1_000_000, transcendentals=0
        ),
    )(src, link, vec, elem)

    def placed(out):
        return out.reshape(1, 2, nsrc, 4, modes_dev).transpose(0, 1, 3, 2, 4)

    return placed(proj), placed(cont)


def solution(mesh):
    placed = (
        P("tm", None, None, None, None, "space", None),
        P(None, "tm", None, None, None, "space", None),
        P("tm", None, None, None, "space", None),
        P("tm", None, "space", None),
    )
    return jax.shard_map(
        local,
        mesh=mesh,
        in_specs=placed,
        out_specs=(P("tm", None, None, None, "space"), P("tm", None, None, None, "space")),
        check_vma=False,
    )
```

```python
import functools

import jax
import jax.numpy as jnp
from jax import lax
from jax.experimental import pallas as pl
from jax.experimental.pallas import tpu as pltpu
from jax.sharding import PartitionSpec as P

LX = 8
HOPPING = 0.125
SWEEPS = 3
GROUP = 4
MESH = pl.DeviceIdType.MESH
f32 = jnp.float32
bf16 = jnp.bfloat16


def each(lower, upper, body):
    if upper - lower <= 16:
        for index in range(lower, upper):
            body(index)
    else:
        lax.fori_loop(lower, upper, lambda index, carry: (body(index), carry)[1], 0)


def kernel(
    slices, peers, nsrc, modes_dev,
    src_hbm, link_hbm, vec_hbm, elem_hbm,
    turned,
    src_in, link_in, vec_in, elem_in, load_sem,
    wide, link_wide, links, base, field, hops, vec_wide,
    halo_out, halo_in, halo_send, halo_recv,
    elem_all, elem_full, elem_send, elem_recv,
    left_mat, right_mat, sums, part_out, part_in, part_send, part_recv,
):
    groups = nsrc // GROUP
    half = 2 * GROUP
    lanes = base.shape[-1]
    nmode = peers * modes_dev
    t = lax.axis_index("tm")
    me = lax.axis_index("space")
    t_up, t_down = lax.rem(t + 1, slices), lax.rem(t + slices - 1, slices)
    z_up, z_down = lax.rem(me + 1, peers), lax.rem(me + peers - 1, peers)

    barrier = pltpu.get_barrier_semaphore()

    def greet(off):
        pl.semaphore_signal(
            barrier, inc=1, device_id=(t, lax.rem(me + off, peers)), device_id_type=MESH
        )

    for near in (t_up, t_down):
        pl.semaphore_signal(barrier, inc=1, device_id=(near, me), device_id_type=MESH)
    each(1, peers, greet)

    loads = [
        pltpu.make_async_copy(a, b, load_sem.at[i])
        for i, (a, b) in enumerate(
            ((src_hbm, src_in), (link_hbm, link_in), (elem_hbm, elem_in), (vec_hbm, vec_in))
        )
    ]
    for load in loads:
        load.start()

    row_at = lax.broadcasted_iota(jnp.int32, (1, half, lanes), 1)
    spin_sign = jnp.where(row_at < GROUP, 1.0, -1.0).astype(f32)
    column = lax.broadcasted_iota(jnp.int32, (1, half, lanes), 2) % LX
    ahead_sign = jnp.where(t == slices - 1, -1.0, 1.0).astype(f32)
    behind_sign = jnp.where(t == 0, -1.0, 1.0).astype(f32)

    def apply(mu, pair, dagger):
        re, im = pair
        out_re = out_im = None
        for j in range(3):
            if dagger:
                g_re, g_im = links[mu, 0, j], links[mu, 1, j]
            else:
                g_re, g_im = links[mu, 0, :, j], links[mu, 1, :, j]
            v_re, v_im = re[j][None], im[j][None]
            if dagger:
                add_re, add_im = g_re * v_re + g_im * v_im, g_re * v_im - g_im * v_re
            else:
                add_re, add_im = g_re * v_re - g_im * v_im, g_re * v_im + g_im * v_re
            out_re = add_re if out_re is None else out_re + add_re
            out_im = add_im if out_im is None else out_im + add_im
        return out_re, out_im

    def shift(pair, direction, ahead):
        out = []
        for v in pair:
            if direction == 1:
                out.append(pltpu.roll(v, lanes - LX if ahead else LX, 2))
            else:
                near = pltpu.roll(v, lanes - 1 if ahead else 1, 2)
                wrap = pltpu.roll(v, LX - 1 if ahead else lanes - LX + 1, 2)
                out.append(jnp.where(column == (LX - 1 if ahead else 0), wrap, near))
        return tuple(out)

    def packed(pair):
        return jnp.concatenate([v.reshape(3 * half, lanes) for v in pair], 0).astype(bf16)

    def unpacked(value):
        value = value.astype(f32).reshape(6, half, lanes)
        return value[:3], value[3:]

    def halo(sweep, g, way):
        at = (sweep * groups + g) * 4 + way
        target = ((t_down, me), (t_up, me), (t, z_down), (t, z_up))[way]
        return pltpu.make_async_remote_copy(
            src_ref=halo_out.at[at],
            dst_ref=halo_in.at[at],
            send_sem=halo_send.at[at],
            recv_sem=halo_recv.at[at],
            device_id=target,
            device_id_type=MESH,
        )

    def send(sweep, g, way, pair):
        halo_out[(sweep * groups + g) * 4 + way] = packed(pair)
        halo(sweep, g, way).start()

    def receive(sweep, g, way):
        halo(sweep, g, way).wait_recv()
        return unpacked(halo_in[(sweep * groups + g) * 4 + way])

    def elem_copy(to, slot):
        return pltpu.make_async_remote_copy(
            src_ref=elem_all.at[me],
            dst_ref=elem_all.at[slot],
            send_sem=elem_send.at[to],
            recv_sem=elem_recv.at[slot],
            device_id=(t, to),
            device_id_type=MESH,
        )

    def part_copy(to, slot):
        return pltpu.make_async_remote_copy(
            src_ref=part_out.at[to],
            dst_ref=part_in.at[slot],
            send_sem=part_send.at[to],
            recv_sem=part_recv.at[slot],
            device_id=(t, to),
            device_id_type=MESH,
        )

    def parts_of(g):
        up = [field[g, 3 * i : 3 * i + 3, 0:half, :] for i in range(2)]
        low = [field[g, 3 * i : 3 * i + 3, half : 2 * half, :] for i in range(2)]
        return up, low

    def turn_z(low):
        return spin_sign * low[1], -(spin_sign * low[0])

    def send_z(sweep, g, minus, plus):
        up, low = parts_of(g)
        turn = turn_z(low)
        if minus:
            send(sweep, g, 2, (up[0] - turn[0], up[1] - turn[1]))
        if plus:
            send(sweep, g, 3, apply(2, (up[0] + turn[0], up[1] + turn[1]), True))

    def send_t(sweep, g, minus, plus):
        up, low = parts_of(g)
        if minus:
            send(sweep, g, 0, (up[0] - low[0], up[1] - low[1]))
        if plus:
            send(sweep, g, 1, apply(3, (up[0] + low[0], up[1] + low[1]), True))

    def plane(g):
        up, low = parts_of(g)
        swapped = [pltpu.roll(v, GROUP, 1) for v in low]
        turned_x = (swapped[1], -swapped[0])
        turned_y = (-(spin_sign * swapped[0]), -(spin_sign * swapped[1]))
        ahead = {}
        behind = {}
        for mu, moved in ((0, turned_x), (1, turned_y)):
            ahead[mu] = apply(
                mu, shift((up[0] - moved[0], up[1] - moved[1]), mu, True), False
            )
            behind[mu] = shift(
                apply(mu, (up[0] + moved[0], up[1] + moved[1]), True), mu, False
            )
        dx = [behind[0][i] - ahead[0][i] for i in range(2)]
        dy = [behind[1][i] - ahead[1][i] for i in range(2)]
        cross = (-dx[1] - spin_sign * dy[0], dx[0] - spin_sign * dy[1])
        for i in range(2):
            hops[g, i] = ahead[0][i] + behind[0][i] + ahead[1][i] + behind[1][i]
            hops[g, 2 + i] = pltpu.roll(cross[i], GROUP, 1)

    def finish(sweep, g):
        f_t = apply(3, receive(sweep, g, 0), False)
        b_t = receive(sweep, g, 1)
        f_t = [ahead_sign * v for v in f_t]
        b_t = [behind_sign * v for v in b_t]
        f_z = apply(2, receive(sweep, g, 2), False)
        b_z = receive(sweep, g, 3)
        dz = [b_z[i] - f_z[i] for i in range(2)]
        upper = [hops[g, i] + f_t[i] + b_t[i] + f_z[i] + b_z[i] for i in range(2)]
        lower = [hops[g, 2 + i] + b_t[i] - f_t[i] for i in range(2)]
        lower = [lower[0] - spin_sign * dz[1], lower[1] + spin_sign * dz[0]]
        for i in range(2):
            at = slice(3 * i, 3 * i + 3)
            new_up = base[g, at, 0:half, :] + HOPPING * upper[i]
            new_low = base[g, at, half : 2 * half, :] + HOPPING * lower[i]
            field[g, at, 0:half, :] = new_up.astype(bf16).astype(f32)
            field[g, at, half : 2 * half, :] = new_low.astype(bf16).astype(f32)

    loads[0].wait()
    wide[...] = src_in[...].astype(f32)
    for g in range(groups):
        for pc in range(6):
            for spin in range(4):
                piece = wide[pl.ds((pc * nsrc + g * GROUP) * 4 + spin, GROUP, stride=4), :]
                base[g, pc, spin * GROUP : (spin + 1) * GROUP, :] = piece
                field[g, pc, spin * GROUP : (spin + 1) * GROUP, :] = piece
    pl.semaphore_wait(barrier, peers + 1)
    for g in range(groups):
        send_z(0, g, True, False)
    for g in range(groups):
        send_t(0, g, True, False)

    loads[1].wait()
    link_wide[...] = link_in[...].astype(f32)
    for mu in (2, 3, 0, 1):
        for i in range(3):
            for j in range(3):
                for part in range(2):
                    row = ((mu * 3 + i) * 3 + j) * 2 + part
                    links[mu, part, i, j] = jnp.broadcast_to(
                        link_wide[row : row + 1, :], (half, lanes)
                    )
    for g in range(groups):
        send_z(0, g, False, True)
    for g in range(groups):
        send_t(0, g, False, True)

    loads[2].wait()
    elem_all[me] = elem_in[...].astype(elem_all.dtype)
    each(1, peers, lambda off: elem_copy(lax.rem(me + off, peers), me).start())
    for g in range(groups):
        plane(g)

    loads[3].wait()
    vec_wide[...] = vec_in[...].astype(f32)
    for j in range(6):
        left_mat[0:nmode, j * lanes : (j + 1) * lanes] = vec_wide[
            pl.ds(j, nmode, stride=6), :
        ].astype(bf16)

    for sweep in range(1, SWEEPS):
        for g in range(groups):
            finish(sweep - 1, g)
            send_z(sweep, g, True, True)
            send_t(sweep, g, True, True)
        for g in range(groups):
            plane(g)
        if sweep == 1:
            def arrive(off):
                p = lax.rem(me + off, peers)
                elem_copy(p, p).wait_recv()

            each(1, peers, arrive)
            for p in range(peers):
                for part in range(2):
                    elem_full[part, p * modes_dev : (p + 1) * modes_dev, :] = elem_all[
                        p, part
                    ].astype(f32)
            e_re, e_im = elem_full[0].astype(bf16), elem_full[1].astype(bf16)
            blocks = jnp.concatenate(
                [
                    jnp.concatenate([e_re, e_im], 1),
                    jnp.concatenate([-e_im, e_re], 1),
                ],
                0,
            )
            for c in range(3):
                both = jnp.concatenate(
                    [
                        left_mat[0:nmode, (2 * c + part) * lanes : (2 * c + part + 1) * lanes]
                        for part in range(2)
                    ],
                    0,
                )
                mixed = jnp.dot(blocks, both, preferred_element_type=f32).astype(bf16)
                for part in range(2):
                    left_mat[
                        nmode : 2 * nmode, (2 * c + part) * lanes : (2 * c + part + 1) * lanes
                    ] = mixed[part * nmode : (part + 1) * nmode]

    for g in range(groups):
        finish(SWEEPS - 1, g)
        for pc in range(6):
            for spin in range(4):
                wide[pl.ds((pc * nsrc + g * GROUP) * 4 + spin, GROUP, stride=4), :] = field[
                    g, pc, spin * GROUP : (spin + 1) * GROUP, :
                ]
    count = 4 * nsrc
    for c in range(3):
        re = wide[c * count : (c + 1) * count, :]
        im = wide[(3 + c) * count : (4 + c) * count, :]
        at = 2 * c * lanes
        right_mat[:, at : at + lanes] = jnp.concatenate([re, im], 0).astype(bf16)
        right_mat[:, at + lanes : at + 2 * lanes] = jnp.concatenate([im, -re], 0).astype(bf16)
    sums[:, 0 : 2 * count] = lax.dot_general(
        left_mat[...], right_mat[...], (((1,), (1,)), ((), ())), preferred_element_type=f32
    )
    for p in range(peers):
        for o in range(2):
            at = o * nmode + p * modes_dev
            part_out[p, o] = sums[at : at + modes_dev, :].astype(part_out.dtype)
    each(1, peers, lambda off: part_copy(lax.rem(me + off, peers), me).start())

    turned[...] = jnp.zeros_like(turned)
    for o in range(2):
        turned[o * modes_dev : (o + 1) * modes_dev, :] = part_out[me, o].astype(f32)

    def settle(off):
        p = lax.rem(me + off, peers)
        elem_copy(p, me).wait_send()
        part_copy(p, me).wait_send()

    for sweep in range(SWEEPS):
        for g in range(groups):
            for way in range(4):
                halo(sweep, g, way).wait_send()
    each(1, peers, settle)

    def gather(off):
        p = lax.rem(me + off, peers)
        part_copy(p, p).wait_recv()
        for o in range(2):
            turned[o * modes_dev : (o + 1) * modes_dev, :] += part_in[p, o].astype(f32)

    each(1, peers, gather)


def finish_kernel(turned, proj_ref, cont_ref):
    count, modes_dev = proj_ref.shape
    flipped = turned[...].T
    proj_ref[...] = flipped[0:count, 0:modes_dev]
    cont_ref[...] = flipped[0:count, modes_dev : 2 * modes_dev]


def local(sources, gauge_links, eigenvectors, elementals):
    slices, peers = lax.axis_size("tm"), lax.axis_size("space")
    _, _, _, _, nsrc, _, lanes = sources.shape
    nmode = eigenvectors.shape[1]
    modes_dev = elementals.shape[2]
    src = sources.transpose(0, 1, 3, 4, 5, 2, 6).reshape(24 * nsrc, lanes)
    link = gauge_links.transpose(0, 1, 3, 4, 5, 2, 6).reshape(72, lanes)
    vec = eigenvectors.transpose(0, 1, 3, 4, 2, 5).reshape(6 * nmode, lanes)
    elem = elementals.reshape(2, modes_dev, nmode)
    groups, half = nsrc // GROUP, 2 * GROUP
    halos = SWEEPS * groups * 4
    src, link, vec, elem = [
        pltpu.with_memory_space_constraint(x, pltpu.HBM) for x in (src, link, vec, elem)
    ]
    kind = bf16 if modes_dev % 16 == 0 else f32
    outs = jax.ShapeDtypeStruct((8 * nsrc, modes_dev), f32)
    dma = pltpu.SemaphoreType.DMA
    vmem = pl.BlockSpec(memory_space=pltpu.VMEM)
    turned = pl.pallas_call(
        functools.partial(kernel, slices, peers, nsrc, modes_dev),
        out_shape=jax.ShapeDtypeStruct((128, 128), f32),
        in_specs=[pl.BlockSpec(memory_space=pltpu.HBM)] * 4,
        out_specs=vmem,
        scratch_shapes=[
            pltpu.VMEM(src.shape, bf16),
            pltpu.VMEM(link.shape, bf16),
            pltpu.VMEM(vec.shape, bf16),
            pltpu.VMEM(elem.shape, f32),
            dma((4,)),
            pltpu.VMEM(src.shape, f32),
            pltpu.VMEM(link.shape, f32),
            pltpu.VMEM((4, 2, 3, 3, half, lanes), f32),
            pltpu.VMEM((groups, 6, 2 * half, lanes), f32),
            pltpu.VMEM((groups, 6, 2 * half, lanes), f32),
            pltpu.VMEM((groups, 4, 3, half, lanes), f32),
            pltpu.VMEM(vec.shape, f32),
            pltpu.VMEM((halos, 6 * half, lanes), bf16),
            pltpu.VMEM((halos, 6 * half, lanes), bf16),
            dma((halos,)),
            dma((halos,)),
            pltpu.VMEM((peers, 2, modes_dev, nmode), kind),
            pltpu.VMEM((2, nmode, nmode), f32),
            dma((peers,)),
            dma((peers,)),
            pltpu.VMEM((2 * nmode, 6 * lanes), bf16),
            pltpu.VMEM((8 * nsrc, 6 * lanes), bf16),
            pltpu.VMEM((2 * nmode, 128), f32),
            pltpu.VMEM((peers, 2, modes_dev, 128), kind),
            pltpu.VMEM((peers, 2, modes_dev, 128), kind),
            dma((peers,)),
            dma((peers,)),
        ],
        compiler_params=pltpu.CompilerParams(
            collective_id=0, has_side_effects=True, vmem_limit_bytes=32 * 1024 * 1024
        ),
        cost_estimate=pl.CostEstimate(
            flops=200_000_000, bytes_accessed=1_000_000, transcendentals=0
        ),
    )(src, link, vec, elem)
    proj, cont = pl.pallas_call(
        finish_kernel, out_shape=(outs, outs), in_specs=[vmem], out_specs=[vmem] * 2
    )(turned)

    def placed(out):
        return out.reshape(1, 2, nsrc, 4, modes_dev).transpose(0, 1, 3, 2, 4)

    return placed(proj), placed(cont)


def solution(mesh):
    placed = (
        P("tm", None, None, None, None, "space", None),
        P(None, "tm", None, None, None, "space", None),
        P("tm", None, None, None, "space", None),
        P("tm", None, "space", None),
    )
    return jax.shard_map(
        local,
        mesh=mesh,
        in_specs=placed,
        out_specs=(P("tm", None, None, None, "space"), P("tm", None, None, None, "space")),
        check_vma=False,
    )
```

```python
import functools

import jax
import jax.numpy as jnp
from jax import lax
from jax.experimental import pallas as pl
from jax.experimental.pallas import tpu as pltpu
from jax.sharding import PartitionSpec as P

LX = 8
HOPPING = 0.125
SWEEPS = 3
GROUP = 4
MESH = pl.DeviceIdType.MESH
f32 = jnp.float32
bf16 = jnp.bfloat16


def each(lower, upper, body):
    if upper - lower <= 16:
        for index in range(lower, upper):
            body(index)
    else:
        lax.fori_loop(lower, upper, lambda index, carry: (body(index), carry)[1], 0)


def kernel(
    slices, peers, nsrc, modes_dev,
    src_hbm, link_hbm, vec_hbm, elem_hbm,
    proj_ref, cont_ref,
    src_in, link_in, vec_in, elem_in, load_sem,
    wide, link_wide, links, base, field, hops, vec_wide,
    halo_out, halo_in, halo_send, halo_recv,
    elem_all, elem_full, elem_send, elem_recv,
    left_mat, right_mat, sums, part_out, part_in, part_send, part_recv, turned,
):
    groups = nsrc // GROUP
    half = 2 * GROUP
    lanes = base.shape[-1]
    nmode = peers * modes_dev
    t = lax.axis_index("tm")
    me = lax.axis_index("space")
    t_up, t_down = lax.rem(t + 1, slices), lax.rem(t + slices - 1, slices)
    z_up, z_down = lax.rem(me + 1, peers), lax.rem(me + peers - 1, peers)

    barrier = pltpu.get_barrier_semaphore()

    def greet(off):
        pl.semaphore_signal(
            barrier, inc=1, device_id=(t, lax.rem(me + off, peers)), device_id_type=MESH
        )

    for near in (t_up, t_down):
        pl.semaphore_signal(barrier, inc=1, device_id=(near, me), device_id_type=MESH)
    each(1, peers, greet)

    loads = [
        pltpu.make_async_copy(a, b, load_sem.at[i])
        for i, (a, b) in enumerate(
            ((src_hbm, src_in), (link_hbm, link_in), (elem_hbm, elem_in), (vec_hbm, vec_in))
        )
    ]
    for load in loads:
        load.start()

    row_at = lax.broadcasted_iota(jnp.int32, (1, half, lanes), 1)
    spin_sign = jnp.where(row_at < GROUP, 1.0, -1.0).astype(f32)
    column = lax.broadcasted_iota(jnp.int32, (1, half, lanes), 2) % LX
    ahead_sign = jnp.where(t == slices - 1, -1.0, 1.0).astype(f32)
    behind_sign = jnp.where(t == 0, -1.0, 1.0).astype(f32)

    def apply(mu, pair, dagger):
        re, im = pair
        out_re = out_im = None
        for j in range(3):
            if dagger:
                g_re, g_im = links[mu, 0, j], links[mu, 1, j]
            else:
                g_re, g_im = links[mu, 0, :, j], links[mu, 1, :, j]
            v_re, v_im = re[j][None], im[j][None]
            if dagger:
                add_re, add_im = g_re * v_re + g_im * v_im, g_re * v_im - g_im * v_re
            else:
                add_re, add_im = g_re * v_re - g_im * v_im, g_re * v_im + g_im * v_re
            out_re = add_re if out_re is None else out_re + add_re
            out_im = add_im if out_im is None else out_im + add_im
        return out_re, out_im

    def shift(pair, direction, ahead):
        out = []
        for v in pair:
            if direction == 1:
                out.append(pltpu.roll(v, lanes - LX if ahead else LX, 2))
            else:
                near = pltpu.roll(v, lanes - 1 if ahead else 1, 2)
                wrap = pltpu.roll(v, LX - 1 if ahead else lanes - LX + 1, 2)
                out.append(jnp.where(column == (LX - 1 if ahead else 0), wrap, near))
        return tuple(out)

    def packed(pair):
        return jnp.concatenate([v.reshape(3 * half, lanes) for v in pair], 0).astype(bf16)

    def unpacked(value):
        value = value.astype(f32).reshape(6, half, lanes)
        return value[:3], value[3:]

    def halo(sweep, g, way):
        at = (sweep * groups + g) * 4 + way
        target = ((t_down, me), (t_up, me), (t, z_down), (t, z_up))[way]
        return pltpu.make_async_remote_copy(
            src_ref=halo_out.at[at],
            dst_ref=halo_in.at[at],
            send_sem=halo_send.at[at],
            recv_sem=halo_recv.at[at],
            device_id=target,
            device_id_type=MESH,
        )

    def send(sweep, g, way, pair):
        halo_out[(sweep * groups + g) * 4 + way] = packed(pair)
        halo(sweep, g, way).start()

    def receive(sweep, g, way):
        halo(sweep, g, way).wait_recv()
        return unpacked(halo_in[(sweep * groups + g) * 4 + way])

    def elem_copy(to, slot):
        return pltpu.make_async_remote_copy(
            src_ref=elem_all.at[me],
            dst_ref=elem_all.at[slot],
            send_sem=elem_send.at[to],
            recv_sem=elem_recv.at[slot],
            device_id=(t, to),
            device_id_type=MESH,
        )

    def part_copy(to, slot):
        return pltpu.make_async_remote_copy(
            src_ref=part_out.at[to],
            dst_ref=part_in.at[slot],
            send_sem=part_send.at[to],
            recv_sem=part_recv.at[slot],
            device_id=(t, to),
            device_id_type=MESH,
        )

    def parts_of(g):
        up = [field[g, 3 * i : 3 * i + 3, 0:half, :] for i in range(2)]
        low = [field[g, 3 * i : 3 * i + 3, half : 2 * half, :] for i in range(2)]
        return up, low

    def turn_z(low):
        return spin_sign * low[1], -(spin_sign * low[0])

    def send_z(sweep, g, minus, plus):
        up, low = parts_of(g)
        turn = turn_z(low)
        if minus:
            send(sweep, g, 2, (up[0] - turn[0], up[1] - turn[1]))
        if plus:
            send(sweep, g, 3, apply(2, (up[0] + turn[0], up[1] + turn[1]), True))

    def send_t(sweep, g, minus, plus):
        up, low = parts_of(g)
        if minus:
            send(sweep, g, 0, (up[0] - low[0], up[1] - low[1]))
        if plus:
            send(sweep, g, 1, apply(3, (up[0] + low[0], up[1] + low[1]), True))

    def plane(g):
        up, low = parts_of(g)
        swapped = [pltpu.roll(v, GROUP, 1) for v in low]
        turned_x = (swapped[1], -swapped[0])
        turned_y = (-(spin_sign * swapped[0]), -(spin_sign * swapped[1]))
        ahead = {}
        behind = {}
        for mu, moved in ((0, turned_x), (1, turned_y)):
            ahead[mu] = apply(
                mu, shift((up[0] - moved[0], up[1] - moved[1]), mu, True), False
            )
            behind[mu] = shift(
                apply(mu, (up[0] + moved[0], up[1] + moved[1]), True), mu, False
            )
        dx = [behind[0][i] - ahead[0][i] for i in range(2)]
        dy = [behind[1][i] - ahead[1][i] for i in range(2)]
        cross = (-dx[1] - spin_sign * dy[0], dx[0] - spin_sign * dy[1])
        for i in range(2):
            hops[g, i] = ahead[0][i] + behind[0][i] + ahead[1][i] + behind[1][i]
            hops[g, 2 + i] = pltpu.roll(cross[i], GROUP, 1)

    def finish(sweep, g):
        f_t = apply(3, receive(sweep, g, 0), False)
        b_t = receive(sweep, g, 1)
        f_t = [ahead_sign * v for v in f_t]
        b_t = [behind_sign * v for v in b_t]
        f_z = apply(2, receive(sweep, g, 2), False)
        b_z = receive(sweep, g, 3)
        dz = [b_z[i] - f_z[i] for i in range(2)]
        upper = [hops[g, i] + f_t[i] + b_t[i] + f_z[i] + b_z[i] for i in range(2)]
        lower = [hops[g, 2 + i] + b_t[i] - f_t[i] for i in range(2)]
        lower = [lower[0] - spin_sign * dz[1], lower[1] + spin_sign * dz[0]]
        for i in range(2):
            at = slice(3 * i, 3 * i + 3)
            new_up = base[g, at, 0:half, :] + HOPPING * upper[i]
            new_low = base[g, at, half : 2 * half, :] + HOPPING * lower[i]
            field[g, at, 0:half, :] = new_up.astype(bf16).astype(f32)
            field[g, at, half : 2 * half, :] = new_low.astype(bf16).astype(f32)

    loads[0].wait()
    wide[...] = src_in[...].astype(f32)
    for g in range(groups):
        for pc in range(6):
            for spin in range(4):
                piece = wide[pl.ds((pc * nsrc + g * GROUP) * 4 + spin, GROUP, stride=4), :]
                base[g, pc, spin * GROUP : (spin + 1) * GROUP, :] = piece
                field[g, pc, spin * GROUP : (spin + 1) * GROUP, :] = piece
    pl.semaphore_wait(barrier, peers + 1)
    for g in range(groups):
        send_z(0, g, True, False)
    for g in range(groups):
        send_t(0, g, True, False)

    loads[1].wait()
    link_wide[...] = link_in[...].astype(f32)
    for mu in (2, 3, 0, 1):
        for i in range(3):
            for j in range(3):
                for part in range(2):
                    row = ((mu * 3 + i) * 3 + j) * 2 + part
                    links[mu, part, i, j] = jnp.broadcast_to(
                        link_wide[row : row + 1, :], (half, lanes)
                    )
    for g in range(groups):
        send_z(0, g, False, True)
    for g in range(groups):
        send_t(0, g, False, True)

    loads[2].wait()
    elem_all[me] = elem_in[...].astype(elem_all.dtype)
    each(1, peers, lambda off: elem_copy(lax.rem(me + off, peers), me).start())
    for g in range(groups):
        plane(g)

    loads[3].wait()
    vec_wide[...] = vec_in[...].astype(f32)
    for j in range(6):
        left_mat[0:nmode, j * lanes : (j + 1) * lanes] = vec_wide[
            pl.ds(j, nmode, stride=6), :
        ].astype(bf16)

    for sweep in range(1, SWEEPS):
        for g in range(groups):
            finish(sweep - 1, g)
            send_z(sweep, g, True, True)
            send_t(sweep, g, True, True)
        for g in range(groups):
            plane(g)
        if sweep == 1:
            def arrive(off):
                p = lax.rem(me + off, peers)
                elem_copy(p, p).wait_recv()

            each(1, peers, arrive)
            for p in range(peers):
                for part in range(2):
                    elem_full[part, p * modes_dev : (p + 1) * modes_dev, :] = elem_all[
                        p, part
                    ].astype(f32)
            e_re, e_im = elem_full[0].astype(bf16), elem_full[1].astype(bf16)
            blocks = jnp.concatenate(
                [
                    jnp.concatenate([e_re, e_im], 1),
                    jnp.concatenate([-e_im, e_re], 1),
                ],
                0,
            )
            for c in range(3):
                both = jnp.concatenate(
                    [
                        left_mat[0:nmode, (2 * c + part) * lanes : (2 * c + part + 1) * lanes]
                        for part in range(2)
                    ],
                    0,
                )
                mixed = jnp.dot(blocks, both, preferred_element_type=f32).astype(bf16)
                for part in range(2):
                    left_mat[
                        nmode : 2 * nmode, (2 * c + part) * lanes : (2 * c + part + 1) * lanes
                    ] = mixed[part * nmode : (part + 1) * nmode]

    count = 4 * nsrc
    chunk = 4 * GROUP
    for g in range(groups):
        finish(SWEEPS - 1, g)
        for pc in range(6):
            for spin in range(4):
                wide[pl.ds((g * 6 + pc) * chunk + spin, GROUP, stride=4), :] = field[
                    g, pc, spin * GROUP : (spin + 1) * GROUP, :
                ]
        rows = slice(2 * g * chunk, 2 * (g + 1) * chunk)
        for c in range(3):
            re_at, im_at = (g * 6 + c) * chunk, (g * 6 + 3 + c) * chunk
            re, im = wide[re_at : re_at + chunk, :], wide[im_at : im_at + chunk, :]
            at = 2 * c * lanes
            right_mat[rows, at : at + lanes] = jnp.concatenate([re, im], 0).astype(bf16)
            right_mat[rows, at + lanes : at + 2 * lanes] = jnp.concatenate(
                [im, -re], 0
            ).astype(bf16)
    sums[:, 0 : 2 * count] = lax.dot_general(
        left_mat[...], right_mat[...], (((1,), (1,)), ((), ())), preferred_element_type=f32
    )
    for p in range(peers):
        for o in range(2):
            at = o * nmode + p * modes_dev
            part_out[p, o] = sums[at : at + modes_dev, :].astype(part_out.dtype)
    each(1, peers, lambda off: part_copy(lax.rem(me + off, peers), me).start())

    turned[...] = jnp.zeros_like(turned)
    for o in range(2):
        turned[o * modes_dev : (o + 1) * modes_dev, :] = part_out[me, o].astype(f32)

    def settle(off):
        p = lax.rem(me + off, peers)
        elem_copy(p, me).wait_send()
        part_copy(p, me).wait_send()

    for sweep in range(SWEEPS):
        for g in range(groups):
            for way in range(4):
                halo(sweep, g, way).wait_send()
    each(1, peers, settle)

    def gather(off):
        p = lax.rem(me + off, peers)
        part_copy(p, p).wait_recv()
        for o in range(2):
            turned[o * modes_dev : (o + 1) * modes_dev, :] += part_in[p, o].astype(f32)

    each(1, peers, gather)
    flipped = turned[...].T
    for g in range(groups):
        for part in range(2):
            got = flipped[(2 * g + part) * chunk : (2 * g + part + 1) * chunk]
            to = slice(part * count + g * chunk, part * count + (g + 1) * chunk)
            proj_ref[to, :] = got[:, 0:modes_dev]
            cont_ref[to, :] = got[:, modes_dev : 2 * modes_dev]


def local(sources, gauge_links, eigenvectors, elementals):
    slices, peers = lax.axis_size("tm"), lax.axis_size("space")
    _, _, _, _, nsrc, _, lanes = sources.shape
    nmode = eigenvectors.shape[1]
    modes_dev = elementals.shape[2]
    src = sources.transpose(0, 1, 3, 4, 5, 2, 6).reshape(24 * nsrc, lanes)
    link = gauge_links.transpose(0, 1, 3, 4, 5, 2, 6).reshape(72, lanes)
    vec = eigenvectors.transpose(0, 1, 3, 4, 2, 5).reshape(6 * nmode, lanes)
    elem = elementals.reshape(2, modes_dev, nmode)
    groups, half = nsrc // GROUP, 2 * GROUP
    halos = SWEEPS * groups * 4
    src, link, vec, elem = [
        pltpu.with_memory_space_constraint(x, pltpu.HBM) for x in (src, link, vec, elem)
    ]
    kind = bf16 if modes_dev % 16 == 0 else f32
    outs = jax.ShapeDtypeStruct((8 * nsrc, modes_dev), f32)
    dma = pltpu.SemaphoreType.DMA
    vmem = pl.BlockSpec(memory_space=pltpu.VMEM)
    proj, cont = pl.pallas_call(
        functools.partial(kernel, slices, peers, nsrc, modes_dev),
        out_shape=(outs, outs),
        in_specs=[pl.BlockSpec(memory_space=pltpu.HBM)] * 4,
        out_specs=[vmem] * 2,
        scratch_shapes=[
            pltpu.VMEM(src.shape, bf16),
            pltpu.VMEM(link.shape, bf16),
            pltpu.VMEM(vec.shape, bf16),
            pltpu.VMEM(elem.shape, f32),
            dma((4,)),
            pltpu.VMEM(src.shape, f32),
            pltpu.VMEM(link.shape, f32),
            pltpu.VMEM((4, 2, 3, 3, half, lanes), f32),
            pltpu.VMEM((groups, 6, 2 * half, lanes), f32),
            pltpu.VMEM((groups, 6, 2 * half, lanes), f32),
            pltpu.VMEM((groups, 4, 3, half, lanes), f32),
            pltpu.VMEM(vec.shape, f32),
            pltpu.VMEM((halos, 6 * half, lanes), bf16),
            pltpu.VMEM((halos, 6 * half, lanes), bf16),
            dma((halos,)),
            dma((halos,)),
            pltpu.VMEM((peers, 2, modes_dev, nmode), kind),
            pltpu.VMEM((2, nmode, nmode), f32),
            dma((peers,)),
            dma((peers,)),
            pltpu.VMEM((2 * nmode, 6 * lanes), bf16),
            pltpu.VMEM((8 * nsrc, 6 * lanes), bf16),
            pltpu.VMEM((2 * nmode, 128), f32),
            pltpu.VMEM((peers, 2, modes_dev, 128), kind),
            pltpu.VMEM((peers, 2, modes_dev, 128), kind),
            dma((peers,)),
            dma((peers,)),
            pltpu.VMEM((128, 128), f32),
        ],
        compiler_params=pltpu.CompilerParams(
            collective_id=0, has_side_effects=True, vmem_limit_bytes=32 * 1024 * 1024
        ),
        cost_estimate=pl.CostEstimate(
            flops=200_000_000, bytes_accessed=1_000_000, transcendentals=0
        ),
    )(src, link, vec, elem)

    def placed(out):
        return out.reshape(1, 2, nsrc, 4, modes_dev).transpose(0, 1, 3, 2, 4)

    return placed(proj), placed(cont)


def solution(mesh):
    placed = (
        P("tm", None, None, None, None, "space", None),
        P(None, "tm", None, None, None, "space", None),
        P("tm", None, None, None, "space", None),
        P("tm", None, "space", None),
    )
    return jax.shard_map(
        local,
        mesh=mesh,
        in_specs=placed,
        out_specs=(P("tm", None, None, None, "space"), P("tm", None, None, None, "space")),
        check_vma=False,
    )
```

```python
import functools

import jax
import jax.numpy as jnp
from jax import lax
from jax.experimental import pallas as pl
from jax.experimental.pallas import tpu as pltpu
from jax.sharding import PartitionSpec as P

LX = 8
HOPPING = 0.125
SWEEPS = 3
GROUP = 4
MESH = pl.DeviceIdType.MESH
f32 = jnp.float32
bf16 = jnp.bfloat16


def each(lower, upper, body):
    lax.fori_loop(lower, upper, lambda index, carry: (body(index), carry)[1], 0)


def loop(count, body):
    each(0, count, body)


def kernel(
    slices, peers, nsrc, modes_dev,
    src_hbm, link_hbm, vec_hbm, elem_hbm,
    proj_ref, cont_ref,
    src_in, link_in, vec_in, elem_in, load_sem,
    wide, link_wide, links, base, field, hops, vec_wide,
    halo_out, halo_in, halo_send, halo_recv,
    elem_all, elem_full, elem_send, elem_recv,
    left_mat, right_mat, sums, part_out, part_in, part_send, part_recv, turned,
):
    groups = nsrc // GROUP
    half = 2 * GROUP
    lanes = base.shape[-1]
    nmode = peers * modes_dev
    t = lax.axis_index("tm")
    me = lax.axis_index("space")
    t_up, t_down = lax.rem(t + 1, slices), lax.rem(t + slices - 1, slices)
    z_up, z_down = lax.rem(me + 1, peers), lax.rem(me + peers - 1, peers)

    barrier = pltpu.get_barrier_semaphore()

    loads = [
        pltpu.make_async_copy(a, b, load_sem.at[i])
        for i, (a, b) in enumerate(
            ((src_hbm, src_in), (link_hbm, link_in), (elem_hbm, elem_in), (vec_hbm, vec_in))
        )
    ]
    for load in loads:
        load.start()

    def greet(off):
        pl.semaphore_signal(
            barrier, inc=1, device_id=(t, lax.rem(me + off, peers)), device_id_type=MESH
        )

    for near in (t_up, t_down):
        pl.semaphore_signal(barrier, inc=1, device_id=(near, me), device_id_type=MESH)
    each(1, peers, greet)

    row_at = lax.broadcasted_iota(jnp.int32, (1, half, lanes), 1)
    spin_sign = jnp.where(row_at < GROUP, 1.0, -1.0).astype(f32)
    column = lax.broadcasted_iota(jnp.int32, (1, half, lanes), 2) % LX
    ahead_sign = jnp.where(t == slices - 1, -1.0, 1.0).astype(f32)
    behind_sign = jnp.where(t == 0, -1.0, 1.0).astype(f32)

    def apply(mu, pair, dagger):
        re, im = pair
        out_re = out_im = None
        for j in range(3):
            if dagger:
                g_re, g_im = links[mu, 0, j], links[mu, 1, j]
            else:
                g_re, g_im = links[mu, 0, :, j], links[mu, 1, :, j]
            v_re, v_im = re[j][None], im[j][None]
            if dagger:
                add_re, add_im = g_re * v_re + g_im * v_im, g_re * v_im - g_im * v_re
            else:
                add_re, add_im = g_re * v_re - g_im * v_im, g_re * v_im + g_im * v_re
            out_re = add_re if out_re is None else out_re + add_re
            out_im = add_im if out_im is None else out_im + add_im
        return out_re, out_im

    def shift(pair, direction, ahead):
        out = []
        for v in pair:
            if direction == 1:
                out.append(pltpu.roll(v, lanes - LX if ahead else LX, 2))
            else:
                near = pltpu.roll(v, lanes - 1 if ahead else 1, 2)
                wrap = pltpu.roll(v, LX - 1 if ahead else lanes - LX + 1, 2)
                out.append(jnp.where(column == (LX - 1 if ahead else 0), wrap, near))
        return tuple(out)

    def packed(pair):
        return jnp.concatenate([v.reshape(3 * half, lanes) for v in pair], 0).astype(bf16)

    def unpacked(value):
        value = value.astype(f32).reshape(6, half, lanes)
        return value[:3], value[3:]

    def halo(sweep, g, way):
        at = (sweep * groups + g) * 4 + way
        target = ((t_down, me), (t_up, me), (t, z_down), (t, z_up))[way]
        return pltpu.make_async_remote_copy(
            src_ref=halo_out.at[at],
            dst_ref=halo_in.at[at],
            send_sem=halo_send.at[at],
            recv_sem=halo_recv.at[at],
            device_id=target,
            device_id_type=MESH,
        )

    def send(sweep, g, way, pair):
        halo_out[(sweep * groups + g) * 4 + way] = packed(pair)
        halo(sweep, g, way).start()

    def receive(sweep, g, way):
        halo(sweep, g, way).wait_recv()
        return unpacked(halo_in[(sweep * groups + g) * 4 + way])

    def elem_copy(to, slot):
        return pltpu.make_async_remote_copy(
            src_ref=elem_all.at[me],
            dst_ref=elem_all.at[slot],
            send_sem=elem_send.at[to],
            recv_sem=elem_recv.at[slot],
            device_id=(t, to),
            device_id_type=MESH,
        )

    def part_copy(to, slot):
        return pltpu.make_async_remote_copy(
            src_ref=part_out.at[to],
            dst_ref=part_in.at[slot],
            send_sem=part_send.at[to],
            recv_sem=part_recv.at[slot],
            device_id=(t, to),
            device_id_type=MESH,
        )

    def parts_of(g):
        up = [field[g, 3 * i : 3 * i + 3, 0:half, :] for i in range(2)]
        low = [field[g, 3 * i : 3 * i + 3, half : 2 * half, :] for i in range(2)]
        return up, low

    def turn_z(low):
        return spin_sign * low[1], -(spin_sign * low[0])

    def send_z(sweep, g, minus, plus):
        up, low = parts_of(g)
        turn = turn_z(low)
        if minus:
            send(sweep, g, 2, (up[0] - turn[0], up[1] - turn[1]))
        if plus:
            send(sweep, g, 3, apply(2, (up[0] + turn[0], up[1] + turn[1]), True))

    def send_t(sweep, g, minus, plus):
        up, low = parts_of(g)
        if minus:
            send(sweep, g, 0, (up[0] - low[0], up[1] - low[1]))
        if plus:
            send(sweep, g, 1, apply(3, (up[0] + low[0], up[1] + low[1]), True))

    def plane(g):
        up, low = parts_of(g)
        swapped = [pltpu.roll(v, GROUP, 1) for v in low]
        turned_x = (swapped[1], -swapped[0])
        turned_y = (-(spin_sign * swapped[0]), -(spin_sign * swapped[1]))
        ahead = {}
        behind = {}
        for mu, moved in ((0, turned_x), (1, turned_y)):
            ahead[mu] = apply(
                mu, shift((up[0] - moved[0], up[1] - moved[1]), mu, True), False
            )
            behind[mu] = shift(
                apply(mu, (up[0] + moved[0], up[1] + moved[1]), True), mu, False
            )
        dx = [behind[0][i] - ahead[0][i] for i in range(2)]
        dy = [behind[1][i] - ahead[1][i] for i in range(2)]
        cross = (-dx[1] - spin_sign * dy[0], dx[0] - spin_sign * dy[1])
        for i in range(2):
            hops[g, i] = ahead[0][i] + behind[0][i] + ahead[1][i] + behind[1][i]
            hops[g, 2 + i] = pltpu.roll(cross[i], GROUP, 1)

    def finish(sweep, g):
        f_t = apply(3, receive(sweep, g, 0), False)
        b_t = receive(sweep, g, 1)
        f_t = [ahead_sign * v for v in f_t]
        b_t = [behind_sign * v for v in b_t]
        f_z = apply(2, receive(sweep, g, 2), False)
        b_z = receive(sweep, g, 3)
        dz = [b_z[i] - f_z[i] for i in range(2)]
        upper = [hops[g, i] + f_t[i] + b_t[i] + f_z[i] + b_z[i] for i in range(2)]
        lower = [hops[g, 2 + i] + b_t[i] - f_t[i] for i in range(2)]
        lower = [lower[0] - spin_sign * dz[1], lower[1] + spin_sign * dz[0]]
        for i in range(2):
            at = slice(3 * i, 3 * i + 3)
            new_up = base[g, at, 0:half, :] + HOPPING * upper[i]
            new_low = base[g, at, half : 2 * half, :] + HOPPING * lower[i]
            field[g, at, 0:half, :] = new_up.astype(bf16).astype(f32)
            field[g, at, half : 2 * half, :] = new_low.astype(bf16).astype(f32)

    loads[1].wait()
    link_wide[...] = link_in[...].astype(f32)
    for mu in range(4):
        for i in range(3):
            for j in range(3):
                for part in range(2):
                    row = ((mu * 3 + i) * 3 + j) * 2 + part
                    links[mu, part, i, j] = jnp.broadcast_to(
                        link_wide[row : row + 1, :], (half, lanes)
                    )

    loads[0].wait()
    wide[...] = src_in[...].astype(f32)

    def arrange(g):
        for pc in range(6):
            for spin in range(4):
                piece = wide[pl.ds((pc * nsrc + g * GROUP) * 4 + spin, GROUP, stride=4), :]
                base[g, pc, spin * GROUP : (spin + 1) * GROUP, :] = piece
                field[g, pc, spin * GROUP : (spin + 1) * GROUP, :] = piece

    loop(groups, arrange)
    pl.semaphore_wait(barrier, peers + 1)

    def spread():
        loads[2].wait()
        elem_all[me] = elem_in[...].astype(elem_all.dtype)
        each(1, peers, lambda off: elem_copy(lax.rem(me + off, peers), me).start())
        loads[3].wait()
        vec_wide[...] = vec_in[...].astype(f32)
        for j in range(6):
            left_mat[0:nmode, j * lanes : (j + 1) * lanes] = vec_wide[
                pl.ds(j, nmode, stride=6), :
            ].astype(bf16)

    def mix():
        def arrive(off):
            p = lax.rem(me + off, peers)
            elem_copy(p, p).wait_recv()

        each(1, peers, arrive)
        for p in range(peers):
            for part in range(2):
                elem_full[part, p * modes_dev : (p + 1) * modes_dev, :] = elem_all[
                    p, part
                ].astype(f32)
        e_re, e_im = elem_full[0].astype(bf16), elem_full[1].astype(bf16)
        blocks = jnp.concatenate(
            [
                jnp.concatenate([e_re, e_im], 1),
                jnp.concatenate([-e_im, e_re], 1),
            ],
            0,
        )
        for c in range(3):
            both = jnp.concatenate(
                [
                    left_mat[0:nmode, (2 * c + part) * lanes : (2 * c + part + 1) * lanes]
                    for part in range(2)
                ],
                0,
            )
            mixed = jnp.dot(blocks, both, preferred_element_type=f32).astype(bf16)
            for part in range(2):
                left_mat[
                    nmode : 2 * nmode, (2 * c + part) * lanes : (2 * c + part + 1) * lanes
                ] = mixed[part * nmode : (part + 1) * nmode]

    def step(sweep):
        def group(g):
            @pl.when(sweep > 0)
            def _():
                finish(sweep - 1, g)

            send_z(sweep, g, True, True)
            send_t(sweep, g, True, True)

        loop(groups, group)
        pl.when(sweep == 0)(spread)
        loop(groups, plane)
        pl.when(sweep == 1)(mix)

    loop(SWEEPS, step)

    count = 4 * nsrc
    chunk = 4 * GROUP

    def close(g):
        finish(SWEEPS - 1, g)
        for pc in range(6):
            for spin in range(4):
                wide[pl.ds((g * 6 + pc) * chunk + spin, GROUP, stride=4), :] = field[
                    g, pc, spin * GROUP : (spin + 1) * GROUP, :
                ]
        rows = pl.ds(pl.multiple_of(2 * g * chunk, 2 * chunk), 2 * chunk)
        for c in range(3):
            re_at, im_at = [
                pl.multiple_of((g * 6 + 3 * part + c) * chunk, chunk) for part in range(2)
            ]
            re, im = wide[pl.ds(re_at, chunk), :], wide[pl.ds(im_at, chunk), :]
            at = 2 * c * lanes
            right_mat[rows, at : at + lanes] = jnp.concatenate([re, im], 0).astype(bf16)
            right_mat[rows, at + lanes : at + 2 * lanes] = jnp.concatenate(
                [im, -re], 0
            ).astype(bf16)

    loop(groups, close)
    sums[:, 0 : 2 * count] = lax.dot_general(
        left_mat[...], right_mat[...], (((1,), (1,)), ((), ())), preferred_element_type=f32
    )
    for p in range(peers):
        for o in range(2):
            at = o * nmode + p * modes_dev
            part_out[p, o] = sums[at : at + modes_dev, :].astype(part_out.dtype)
    each(1, peers, lambda off: part_copy(lax.rem(me + off, peers), me).start())

    turned[...] = jnp.zeros_like(turned)
    for o in range(2):
        turned[o * modes_dev : (o + 1) * modes_dev, :] = part_out[me, o].astype(f32)

    def settle(off):
        p = lax.rem(me + off, peers)
        elem_copy(p, me).wait_send()
        part_copy(p, me).wait_send()

    def settle_group(index):
        for way in range(4):
            halo(0, index, way).wait_send()

    loop(SWEEPS * groups, settle_group)
    each(1, peers, settle)

    def gather(off):
        p = lax.rem(me + off, peers)
        part_copy(p, p).wait_recv()
        for o in range(2):
            turned[o * modes_dev : (o + 1) * modes_dev, :] += part_in[p, o].astype(f32)

    each(1, peers, gather)
    flipped = turned[...].T
    for g in range(groups):
        for part in range(2):
            got = flipped[(2 * g + part) * chunk : (2 * g + part + 1) * chunk]
            to = slice(part * count + g * chunk, part * count + (g + 1) * chunk)
            proj_ref[to, :] = got[:, 0:modes_dev]
            cont_ref[to, :] = got[:, modes_dev : 2 * modes_dev]


def local(sources, gauge_links, eigenvectors, elementals):
    slices, peers = lax.axis_size("tm"), lax.axis_size("space")
    _, _, _, _, nsrc, _, lanes = sources.shape
    nmode = eigenvectors.shape[1]
    modes_dev = elementals.shape[2]
    src = sources.transpose(0, 1, 3, 4, 5, 2, 6).reshape(24 * nsrc, lanes)
    link = gauge_links.transpose(0, 1, 3, 4, 5, 2, 6).reshape(72, lanes)
    vec = eigenvectors.transpose(0, 1, 3, 4, 2, 5).reshape(6 * nmode, lanes)
    elem = elementals.reshape(2, modes_dev, nmode)
    groups, half = nsrc // GROUP, 2 * GROUP
    halos = SWEEPS * groups * 4
    src, link, vec, elem = [
        pltpu.with_memory_space_constraint(x, pltpu.HBM) for x in (src, link, vec, elem)
    ]
    kind = bf16 if modes_dev % 16 == 0 else f32
    outs = jax.ShapeDtypeStruct((8 * nsrc, modes_dev), f32)
    dma = pltpu.SemaphoreType.DMA
    vmem = pl.BlockSpec(memory_space=pltpu.VMEM)
    proj, cont = pl.pallas_call(
        functools.partial(kernel, slices, peers, nsrc, modes_dev),
        out_shape=(outs, outs),
        in_specs=[pl.BlockSpec(memory_space=pltpu.HBM)] * 4,
        out_specs=[vmem] * 2,
        scratch_shapes=[
            pltpu.VMEM(src.shape, bf16),
            pltpu.VMEM(link.shape, bf16),
            pltpu.VMEM(vec.shape, bf16),
            pltpu.VMEM(elem.shape, f32),
            dma((4,)),
            pltpu.VMEM(src.shape, f32),
            pltpu.VMEM(link.shape, f32),
            pltpu.VMEM((4, 2, 3, 3, half, lanes), f32),
            pltpu.VMEM((groups, 6, 2 * half, lanes), f32),
            pltpu.VMEM((groups, 6, 2 * half, lanes), f32),
            pltpu.VMEM((groups, 4, 3, half, lanes), f32),
            pltpu.VMEM(vec.shape, f32),
            pltpu.VMEM((halos, 6 * half, lanes), bf16),
            pltpu.VMEM((halos, 6 * half, lanes), bf16),
            dma((halos,)),
            dma((halos,)),
            pltpu.VMEM((peers, 2, modes_dev, nmode), kind),
            pltpu.VMEM((2, nmode, nmode), f32),
            dma((peers,)),
            dma((peers,)),
            pltpu.VMEM((2 * nmode, 6 * lanes), bf16),
            pltpu.VMEM((8 * nsrc, 6 * lanes), bf16),
            pltpu.VMEM((2 * nmode, 128), f32),
            pltpu.VMEM((peers, 2, modes_dev, 128), kind),
            pltpu.VMEM((peers, 2, modes_dev, 128), kind),
            dma((peers,)),
            dma((peers,)),
            pltpu.VMEM((128, 128), f32),
        ],
        compiler_params=pltpu.CompilerParams(
            collective_id=0, has_side_effects=True, vmem_limit_bytes=32 * 1024 * 1024
        ),
        cost_estimate=pl.CostEstimate(
            flops=200_000_000, bytes_accessed=1_000_000, transcendentals=0
        ),
    )(src, link, vec, elem)

    def placed(out):
        return out.reshape(1, 2, nsrc, 4, modes_dev).transpose(0, 1, 3, 2, 4)

    return placed(proj), placed(cont)


def solution(mesh):
    placed = (
        P("tm", None, None, None, None, "space", None),
        P(None, "tm", None, None, None, "space", None),
        P("tm", None, None, None, "space", None),
        P("tm", None, "space", None),
    )
    return jax.shard_map(
        local,
        mesh=mesh,
        in_specs=placed,
        out_specs=(P("tm", None, None, None, "space"), P("tm", None, None, None, "space")),
        check_vma=False,
    )
```

```python
import functools

import jax
import jax.numpy as jnp
from jax import lax
from jax.experimental import pallas as pl
from jax.experimental.pallas import tpu as pltpu
from jax.sharding import PartitionSpec as P

LX = 8
HOPPING = 0.125
SWEEPS = 3
GROUP = 4
MESH = pl.DeviceIdType.MESH
f32 = jnp.float32
bf16 = jnp.bfloat16


def each(lower, upper, body):
    lax.fori_loop(lower, upper, lambda index, carry: (body(index), carry)[1], 0)


def loop(count, body):
    each(0, count, body)


def kernel(
    slices, peers, nsrc, modes_dev,
    src_hbm, link_hbm, vec_hbm, elem_hbm,
    proj_ref, cont_ref,
    src_in, link_in, vec_in, elem_in, load_sem,
    wide, link_wide, links, base, field, hops, vec_wide,
    halo_out, halo_in, halo_send, halo_recv,
    elem_all, elem_full, elem_send, elem_recv,
    left_mat, right_mat, sums, part_out, part_in, part_send, part_recv, turned,
):
    groups = nsrc // GROUP
    half = 2 * GROUP
    lanes = base.shape[-1]
    nmode = peers * modes_dev
    t = lax.axis_index("tm")
    me = lax.axis_index("space")
    t_up, t_down = lax.rem(t + 1, slices), lax.rem(t + slices - 1, slices)
    z_up, z_down = lax.rem(me + 1, peers), lax.rem(me + peers - 1, peers)

    barrier = pltpu.get_barrier_semaphore()

    loads = [
        pltpu.make_async_copy(a, b, load_sem.at[i])
        for i, (a, b) in enumerate(
            ((src_hbm, src_in), (link_hbm, link_in), (elem_hbm, elem_in), (vec_hbm, vec_in))
        )
    ]
    for load in loads:
        load.start()

    def greet(off):
        pl.semaphore_signal(
            barrier, inc=1, device_id=(t, lax.rem(me + off, peers)), device_id_type=MESH
        )

    for near in (t_up, t_down):
        pl.semaphore_signal(barrier, inc=1, device_id=(near, me), device_id_type=MESH)
    each(1, peers, greet)

    row_at = lax.broadcasted_iota(jnp.int32, (1, half, lanes), 1)
    spin_sign = jnp.where(row_at < GROUP, 1.0, -1.0).astype(f32)
    column = lax.broadcasted_iota(jnp.int32, (1, half, lanes), 2) % LX
    ahead_sign = jnp.where(t == slices - 1, -1.0, 1.0).astype(f32)
    behind_sign = jnp.where(t == 0, -1.0, 1.0).astype(f32)

    def apply(mu, pair, dagger):
        re, im = pair
        out_re = out_im = None
        for j in range(3):
            if dagger:
                g_re, g_im = links[mu, 0, j], links[mu, 1, j]
            else:
                g_re, g_im = links[mu, 0, :, j], links[mu, 1, :, j]
            v_re, v_im = re[j][None], im[j][None]
            if dagger:
                add_re, add_im = g_re * v_re + g_im * v_im, g_re * v_im - g_im * v_re
            else:
                add_re, add_im = g_re * v_re - g_im * v_im, g_re * v_im + g_im * v_re
            out_re = add_re if out_re is None else out_re + add_re
            out_im = add_im if out_im is None else out_im + add_im
        return out_re, out_im

    def shift(pair, direction, ahead):
        out = []
        for v in pair:
            if direction == 1:
                out.append(pltpu.roll(v, lanes - LX if ahead else LX, 2))
            else:
                near = pltpu.roll(v, lanes - 1 if ahead else 1, 2)
                wrap = pltpu.roll(v, LX - 1 if ahead else lanes - LX + 1, 2)
                out.append(jnp.where(column == (LX - 1 if ahead else 0), wrap, near))
        return tuple(out)

    def packed(pair):
        return jnp.concatenate([v.reshape(3 * half, lanes) for v in pair], 0).astype(bf16)

    def unpacked(value):
        value = value.astype(f32).reshape(6, half, lanes)
        return value[:3], value[3:]

    def halo(sweep, g, way):
        at = (sweep * groups + g) * 4 + way
        target = ((t_down, me), (t_up, me), (t, z_down), (t, z_up))[way]
        return pltpu.make_async_remote_copy(
            src_ref=halo_out.at[at],
            dst_ref=halo_in.at[at],
            send_sem=halo_send.at[at],
            recv_sem=halo_recv.at[at],
            device_id=target,
            device_id_type=MESH,
        )

    def send(sweep, g, way, pair):
        halo_out[(sweep * groups + g) * 4 + way] = packed(pair)
        halo(sweep, g, way).start()

    def receive(sweep, g, way):
        halo(sweep, g, way).wait_recv()
        return unpacked(halo_in[(sweep * groups + g) * 4 + way])

    def elem_copy(to, slot):
        return pltpu.make_async_remote_copy(
            src_ref=elem_all.at[me],
            dst_ref=elem_all.at[slot],
            send_sem=elem_send.at[to],
            recv_sem=elem_recv.at[slot],
            device_id=(t, to),
            device_id_type=MESH,
        )

    def part_copy(wave, to, slot):
        return pltpu.make_async_remote_copy(
            src_ref=part_out.at[wave, to],
            dst_ref=part_in.at[wave, slot],
            send_sem=part_send.at[wave * peers + to],
            recv_sem=part_recv.at[wave * peers + slot],
            device_id=(t, to),
            device_id_type=MESH,
        )

    def parts_of(g):
        up = [field[g, 3 * i : 3 * i + 3, 0:half, :] for i in range(2)]
        low = [field[g, 3 * i : 3 * i + 3, half : 2 * half, :] for i in range(2)]
        return up, low

    def turn_z(low):
        return spin_sign * low[1], -(spin_sign * low[0])

    def send_z(sweep, g, minus, plus):
        up, low = parts_of(g)
        turn = turn_z(low)
        if minus:
            send(sweep, g, 2, (up[0] - turn[0], up[1] - turn[1]))
        if plus:
            send(sweep, g, 3, apply(2, (up[0] + turn[0], up[1] + turn[1]), True))

    def send_t(sweep, g, minus, plus):
        up, low = parts_of(g)
        if minus:
            send(sweep, g, 0, (up[0] - low[0], up[1] - low[1]))
        if plus:
            send(sweep, g, 1, apply(3, (up[0] + low[0], up[1] + low[1]), True))

    def plane(g):
        up, low = parts_of(g)
        swapped = [pltpu.roll(v, GROUP, 1) for v in low]
        turned_x = (swapped[1], -swapped[0])
        turned_y = (-(spin_sign * swapped[0]), -(spin_sign * swapped[1]))
        ahead = {}
        behind = {}
        for mu, moved in ((0, turned_x), (1, turned_y)):
            ahead[mu] = apply(
                mu, shift((up[0] - moved[0], up[1] - moved[1]), mu, True), False
            )
            behind[mu] = shift(
                apply(mu, (up[0] + moved[0], up[1] + moved[1]), True), mu, False
            )
        dx = [behind[0][i] - ahead[0][i] for i in range(2)]
        dy = [behind[1][i] - ahead[1][i] for i in range(2)]
        cross = (-dx[1] - spin_sign * dy[0], dx[0] - spin_sign * dy[1])
        for i in range(2):
            hops[g, i] = ahead[0][i] + behind[0][i] + ahead[1][i] + behind[1][i]
            hops[g, 2 + i] = pltpu.roll(cross[i], GROUP, 1)

    def finish(sweep, g):
        f_t = apply(3, receive(sweep, g, 0), False)
        b_t = receive(sweep, g, 1)
        f_t = [ahead_sign * v for v in f_t]
        b_t = [behind_sign * v for v in b_t]
        f_z = apply(2, receive(sweep, g, 2), False)
        b_z = receive(sweep, g, 3)
        dz = [b_z[i] - f_z[i] for i in range(2)]
        upper = [hops[g, i] + f_t[i] + b_t[i] + f_z[i] + b_z[i] for i in range(2)]
        lower = [hops[g, 2 + i] + b_t[i] - f_t[i] for i in range(2)]
        lower = [lower[0] - spin_sign * dz[1], lower[1] + spin_sign * dz[0]]
        for i in range(2):
            at = slice(3 * i, 3 * i + 3)
            new_up = base[g, at, 0:half, :] + HOPPING * upper[i]
            new_low = base[g, at, half : 2 * half, :] + HOPPING * lower[i]
            field[g, at, 0:half, :] = new_up.astype(bf16).astype(f32)
            field[g, at, half : 2 * half, :] = new_low.astype(bf16).astype(f32)

    loads[1].wait()
    link_wide[...] = link_in[...].astype(f32)
    for mu in range(4):
        for i in range(3):
            for j in range(3):
                for part in range(2):
                    row = ((mu * 3 + i) * 3 + j) * 2 + part
                    links[mu, part, i, j] = jnp.broadcast_to(
                        link_wide[row : row + 1, :], (half, lanes)
                    )

    loads[0].wait()
    wide[...] = src_in[...].astype(f32)

    def arrange(g):
        for pc in range(6):
            for spin in range(4):
                piece = wide[pl.ds((pc * nsrc + g * GROUP) * 4 + spin, GROUP, stride=4), :]
                base[g, pc, spin * GROUP : (spin + 1) * GROUP, :] = piece
                field[g, pc, spin * GROUP : (spin + 1) * GROUP, :] = piece

    loop(groups, arrange)
    pl.semaphore_wait(barrier, peers + 1)

    def spread():
        loads[2].wait()
        elem_all[me] = elem_in[...].astype(elem_all.dtype)
        each(1, peers, lambda off: elem_copy(lax.rem(me + off, peers), me).start())
        loads[3].wait()
        vec_wide[...] = vec_in[...].astype(f32)
        for j in range(6):
            left_mat[0:nmode, j * lanes : (j + 1) * lanes] = vec_wide[
                pl.ds(j, nmode, stride=6), :
            ].astype(bf16)

    def mix():
        def arrive(off):
            p = lax.rem(me + off, peers)
            elem_copy(p, p).wait_recv()

        each(1, peers, arrive)
        for p in range(peers):
            for part in range(2):
                elem_full[part, p * modes_dev : (p + 1) * modes_dev, :] = elem_all[
                    p, part
                ].astype(f32)
        e_re, e_im = elem_full[0].astype(bf16), elem_full[1].astype(bf16)
        blocks = jnp.concatenate(
            [
                jnp.concatenate([e_re, e_im], 1),
                jnp.concatenate([-e_im, e_re], 1),
            ],
            0,
        )
        for c in range(3):
            both = jnp.concatenate(
                [
                    left_mat[0:nmode, (2 * c + part) * lanes : (2 * c + part + 1) * lanes]
                    for part in range(2)
                ],
                0,
            )
            mixed = jnp.dot(blocks, both, preferred_element_type=f32).astype(bf16)
            for part in range(2):
                left_mat[
                    nmode : 2 * nmode, (2 * c + part) * lanes : (2 * c + part + 1) * lanes
                ] = mixed[part * nmode : (part + 1) * nmode]

    def step(sweep):
        def group(g):
            @pl.when(sweep > 0)
            def _():
                finish(sweep - 1, g)

            send_z(sweep, g, True, True)
            send_t(sweep, g, True, True)

        loop(groups, group)
        pl.when(sweep == 0)(spread)
        loop(groups, plane)
        pl.when(sweep == 1)(mix)

    loop(SWEEPS, step)

    count = 4 * nsrc
    chunk = 4 * GROUP

    def close(g):
        finish(SWEEPS - 1, g)
        for pc in range(6):
            for spin in range(4):
                wide[pl.ds((g * 6 + pc) * chunk + spin, GROUP, stride=4), :] = field[
                    g, pc, spin * GROUP : (spin + 1) * GROUP, :
                ]
        rows = pl.ds(pl.multiple_of(2 * g * chunk, 2 * chunk), 2 * chunk)
        for c in range(3):
            re_at, im_at = [
                pl.multiple_of((g * 6 + 3 * part + c) * chunk, chunk) for part in range(2)
            ]
            re, im = wide[pl.ds(re_at, chunk), :], wide[pl.ds(im_at, chunk), :]
            at = 2 * c * lanes
            right_mat[rows, at : at + lanes] = jnp.concatenate([re, im], 0).astype(bf16)
            right_mat[rows, at + lanes : at + 2 * lanes] = jnp.concatenate(
                [im, -re], 0
            ).astype(bf16)

    early = groups - 1
    waves = ((0, early), (early, groups))
    mid = sums.shape[-1] // 2

    def emit(wave):
        first, last = waves[wave]
        right = right_mat[2 * first * chunk : 2 * last * chunk, :]
        width = 2 * (last - first) * chunk
        for o in range(2):
            sums[wave, :, o * mid : o * mid + width] = lax.dot_general(
                left_mat[o * nmode : (o + 1) * nmode, :],
                right,
                (((1,), (1,)), ((), ())),
                preferred_element_type=f32,
            )
        for p in range(peers):
            part_out[wave, p] = sums[wave, p * modes_dev : (p + 1) * modes_dev, :].astype(
                part_out.dtype
            )
        each(1, peers, lambda off: part_copy(wave, lax.rem(me + off, peers), me).start())

    for wave in range(2):
        each(*waves[wave], close)
        emit(wave)

    turned[...] = jnp.zeros_like(turned)
    for wave in range(2):
        turned[wave * modes_dev : (wave + 1) * modes_dev, :] = part_out[wave, me].astype(f32)

    def settle(off):
        p = lax.rem(me + off, peers)
        elem_copy(p, me).wait_send()
        for wave in range(2):
            part_copy(wave, p, me).wait_send()

    def settle_group(index):
        for way in range(4):
            halo(0, index, way).wait_send()

    loop(SWEEPS * groups, settle_group)
    each(1, peers, settle)

    for wave in range(2):

        def gather(off):
            p = lax.rem(me + off, peers)
            part_copy(wave, p, p).wait_recv()
            turned[wave * modes_dev : (wave + 1) * modes_dev, :] += part_in[wave, p].astype(f32)

        each(1, peers, gather)
    flipped = turned[...].T
    for g in range(groups):
        wave = 1 if g == early else 0
        for part in range(2):
            row = (2 * (g - waves[wave][0]) + part) * chunk
            cols = slice(wave * modes_dev, (wave + 1) * modes_dev)
            to = slice(part * count + g * chunk, part * count + (g + 1) * chunk)
            proj_ref[to, :] = flipped[row : row + chunk, cols]
            cont_ref[to, :] = flipped[mid + row : mid + row + chunk, cols]


def local(sources, gauge_links, eigenvectors, elementals):
    slices, peers = lax.axis_size("tm"), lax.axis_size("space")
    _, _, _, _, nsrc, _, lanes = sources.shape
    nmode = eigenvectors.shape[1]
    modes_dev = elementals.shape[2]
    src = sources.transpose(0, 1, 3, 4, 5, 2, 6).reshape(24 * nsrc, lanes)
    link = gauge_links.transpose(0, 1, 3, 4, 5, 2, 6).reshape(72, lanes)
    vec = eigenvectors.transpose(0, 1, 3, 4, 2, 5).reshape(6 * nmode, lanes)
    elem = elementals.reshape(2, modes_dev, nmode)
    groups, half = nsrc // GROUP, 2 * GROUP
    halos = SWEEPS * groups * 4
    src, link, vec, elem = [
        pltpu.with_memory_space_constraint(x, pltpu.HBM) for x in (src, link, vec, elem)
    ]
    kind = bf16 if modes_dev % 16 == 0 else f32
    outs = jax.ShapeDtypeStruct((8 * nsrc, modes_dev), f32)
    dma = pltpu.SemaphoreType.DMA
    vmem = pl.BlockSpec(memory_space=pltpu.VMEM)
    proj, cont = pl.pallas_call(
        functools.partial(kernel, slices, peers, nsrc, modes_dev),
        out_shape=(outs, outs),
        in_specs=[pl.BlockSpec(memory_space=pltpu.HBM)] * 4,
        out_specs=[vmem] * 2,
        scratch_shapes=[
            pltpu.VMEM(src.shape, bf16),
            pltpu.VMEM(link.shape, bf16),
            pltpu.VMEM(vec.shape, bf16),
            pltpu.VMEM(elem.shape, f32),
            dma((4,)),
            pltpu.VMEM(src.shape, f32),
            pltpu.VMEM(link.shape, f32),
            pltpu.VMEM((4, 2, 3, 3, half, lanes), f32),
            pltpu.VMEM((groups, 6, 2 * half, lanes), f32),
            pltpu.VMEM((groups, 6, 2 * half, lanes), f32),
            pltpu.VMEM((groups, 4, 3, half, lanes), f32),
            pltpu.VMEM(vec.shape, f32),
            pltpu.VMEM((halos, 6 * half, lanes), bf16),
            pltpu.VMEM((halos, 6 * half, lanes), bf16),
            dma((halos,)),
            dma((halos,)),
            pltpu.VMEM((peers, 2, modes_dev, nmode), kind),
            pltpu.VMEM((2, nmode, nmode), f32),
            dma((peers,)),
            dma((peers,)),
            pltpu.VMEM((2 * nmode, 6 * lanes), bf16),
            pltpu.VMEM((8 * nsrc, 6 * lanes), bf16),
            pltpu.VMEM((2, nmode, 128), f32),
            pltpu.VMEM((2, peers, modes_dev, 128), kind),
            pltpu.VMEM((2, peers, modes_dev, 128), kind),
            dma((2 * peers,)),
            dma((2 * peers,)),
            pltpu.VMEM((128, 128), f32),
        ],
        compiler_params=pltpu.CompilerParams(
            collective_id=0, has_side_effects=True, vmem_limit_bytes=32 * 1024 * 1024
        ),
        cost_estimate=pl.CostEstimate(
            flops=200_000_000, bytes_accessed=1_000_000, transcendentals=0
        ),
    )(src, link, vec, elem)

    def placed(out):
        return out.reshape(1, 2, nsrc, 4, modes_dev).transpose(0, 1, 3, 2, 4)

    return placed(proj), placed(cont)


def solution(mesh):
    placed = (
        P("tm", None, None, None, None, "space", None),
        P(None, "tm", None, None, None, "space", None),
        P("tm", None, None, None, "space", None),
        P("tm", None, "space", None),
    )
    return jax.shard_map(
        local,
        mesh=mesh,
        in_specs=placed,
        out_specs=(P("tm", None, None, None, "space"), P("tm", None, None, None, "space")),
        check_vma=False,
    )
```

```python
import functools

import jax
import jax.numpy as jnp
from jax import lax
from jax.experimental import pallas as pl
from jax.experimental.pallas import tpu as pltpu
from jax.sharding import PartitionSpec as P

LX = 8
HOPPING = 0.125
SWEEPS = 3
GROUP = 4
MESH = pl.DeviceIdType.MESH
f32 = jnp.float32
bf16 = jnp.bfloat16


def each(lower, upper, body):
    lax.fori_loop(lower, upper, lambda index, carry: (body(index), carry)[1], 0)


def loop(count, body):
    each(0, count, body)


def kernel(
    slices, peers, nsrc, modes_dev,
    src_hbm, link_hbm, vec_hbm, elem_hbm,
    proj_ref, cont_ref,
    src_in, link_in, vec_in, elem_in, load_sem,
    wide, link_wide, links, base, field, hops, vec_wide,
    halo_out, halo_in, halo_send, halo_recv,
    elem_all, elem_full, elem_send, elem_recv,
    left_mat, right_mat, sums, part_out, part_in, part_send, part_recv, turned,
):
    groups = nsrc // GROUP
    half = 2 * GROUP
    lanes = base.shape[-1]
    nmode = peers * modes_dev
    t = lax.axis_index("tm")
    me = lax.axis_index("space")
    t_up, t_down = lax.rem(t + 1, slices), lax.rem(t + slices - 1, slices)
    z_up, z_down = lax.rem(me + 1, peers), lax.rem(me + peers - 1, peers)

    barrier = pltpu.get_barrier_semaphore()

    loads = [
        pltpu.make_async_copy(a, b, load_sem.at[i])
        for i, (a, b) in enumerate(
            ((src_hbm, src_in), (link_hbm, link_in), (elem_hbm, elem_in), (vec_hbm, vec_in))
        )
    ]
    for load in loads:
        load.start()

    def greet(off):
        pl.semaphore_signal(
            barrier, inc=1, device_id=(t, lax.rem(me + off, peers)), device_id_type=MESH
        )

    for near in (t_up, t_down):
        pl.semaphore_signal(barrier, inc=1, device_id=(near, me), device_id_type=MESH)
    each(1, peers, greet)

    row_at = lax.broadcasted_iota(jnp.int32, (1, half, lanes), 1)
    spin_sign = jnp.where(row_at < GROUP, 1.0, -1.0).astype(f32)
    column = lax.broadcasted_iota(jnp.int32, (1, half, lanes), 2) % LX
    ahead_sign = jnp.where(t == slices - 1, -1.0, 1.0).astype(f32)
    behind_sign = jnp.where(t == 0, -1.0, 1.0).astype(f32)

    def apply(mu, pair, dagger):
        re, im = pair
        out_re = out_im = None
        for j in range(3):
            if dagger:
                g_re, g_im = links[mu, 0, j], links[mu, 1, j]
            else:
                g_re, g_im = links[mu, 0, :, j], links[mu, 1, :, j]
            v_re, v_im = re[j][None], im[j][None]
            if dagger:
                add_re, add_im = g_re * v_re + g_im * v_im, g_re * v_im - g_im * v_re
            else:
                add_re, add_im = g_re * v_re - g_im * v_im, g_re * v_im + g_im * v_re
            out_re = add_re if out_re is None else out_re + add_re
            out_im = add_im if out_im is None else out_im + add_im
        return out_re, out_im

    def shift(pair, direction, ahead):
        out = []
        for v in pair:
            if direction == 1:
                out.append(pltpu.roll(v, lanes - LX if ahead else LX, 2))
            else:
                near = pltpu.roll(v, lanes - 1 if ahead else 1, 2)
                wrap = pltpu.roll(v, LX - 1 if ahead else lanes - LX + 1, 2)
                out.append(jnp.where(column == (LX - 1 if ahead else 0), wrap, near))
        return tuple(out)

    def packed(pair):
        return jnp.concatenate([v.reshape(3 * half, lanes) for v in pair], 0).astype(bf16)

    def unpacked(value):
        value = value.astype(f32).reshape(6, half, lanes)
        return value[:3], value[3:]

    def halo(sweep, g, way):
        at = (sweep * groups + g) * 4 + way
        target = ((t_down, me), (t_up, me), (t, z_down), (t, z_up))[way]
        return pltpu.make_async_remote_copy(
            src_ref=halo_out.at[at],
            dst_ref=halo_in.at[at],
            send_sem=halo_send.at[at],
            recv_sem=halo_recv.at[at],
            device_id=target,
            device_id_type=MESH,
        )

    def send(sweep, g, way, pair):
        halo_out[(sweep * groups + g) * 4 + way] = packed(pair)
        halo(sweep, g, way).start()

    def receive(sweep, g, way):
        halo(sweep, g, way).wait_recv()
        return unpacked(halo_in[(sweep * groups + g) * 4 + way])

    def elem_copy(to, slot):
        return pltpu.make_async_remote_copy(
            src_ref=elem_all.at[me],
            dst_ref=elem_all.at[slot],
            send_sem=elem_send.at[to],
            recv_sem=elem_recv.at[slot],
            device_id=(t, to),
            device_id_type=MESH,
        )

    def part_copy(to, slot):
        return pltpu.make_async_remote_copy(
            src_ref=part_out.at[to],
            dst_ref=part_in.at[slot],
            send_sem=part_send.at[to],
            recv_sem=part_recv.at[slot],
            device_id=(t, to),
            device_id_type=MESH,
        )

    def parts_of(g):
        up = [field[g, 3 * i : 3 * i + 3, 0:half, :] for i in range(2)]
        low = [field[g, 3 * i : 3 * i + 3, half : 2 * half, :] for i in range(2)]
        return up, low

    def turn_z(low):
        return spin_sign * low[1], -(spin_sign * low[0])

    def send_z(sweep, g, minus, plus):
        up, low = parts_of(g)
        turn = turn_z(low)
        if minus:
            send(sweep, g, 2, (up[0] - turn[0], up[1] - turn[1]))
        if plus:
            send(sweep, g, 3, apply(2, (up[0] + turn[0], up[1] + turn[1]), True))

    def send_t(sweep, g, minus, plus):
        up, low = parts_of(g)
        if minus:
            send(sweep, g, 0, (up[0] - low[0], up[1] - low[1]))
        if plus:
            send(sweep, g, 1, apply(3, (up[0] + low[0], up[1] + low[1]), True))

    def plane(g):
        up, low = parts_of(g)
        swapped = [pltpu.roll(v, GROUP, 1) for v in low]
        turned_x = (swapped[1], -swapped[0])
        turned_y = (-(spin_sign * swapped[0]), -(spin_sign * swapped[1]))
        ahead = {}
        behind = {}
        for mu, moved in ((0, turned_x), (1, turned_y)):
            ahead[mu] = apply(
                mu, shift((up[0] - moved[0], up[1] - moved[1]), mu, True), False
            )
            behind[mu] = shift(
                apply(mu, (up[0] + moved[0], up[1] + moved[1]), True), mu, False
            )
        dx = [behind[0][i] - ahead[0][i] for i in range(2)]
        dy = [behind[1][i] - ahead[1][i] for i in range(2)]
        cross = (-dx[1] - spin_sign * dy[0], dx[0] - spin_sign * dy[1])
        for i in range(2):
            hops[g, i] = ahead[0][i] + behind[0][i] + ahead[1][i] + behind[1][i]
            hops[g, 2 + i] = pltpu.roll(cross[i], GROUP, 1)

    def finish(sweep, g):
        f_t = apply(3, receive(sweep, g, 0), False)
        b_t = receive(sweep, g, 1)
        f_t = [ahead_sign * v for v in f_t]
        b_t = [behind_sign * v for v in b_t]
        f_z = apply(2, receive(sweep, g, 2), False)
        b_z = receive(sweep, g, 3)
        dz = [b_z[i] - f_z[i] for i in range(2)]
        upper = [hops[g, i] + f_t[i] + b_t[i] + f_z[i] + b_z[i] for i in range(2)]
        lower = [hops[g, 2 + i] + b_t[i] - f_t[i] for i in range(2)]
        lower = [lower[0] - spin_sign * dz[1], lower[1] + spin_sign * dz[0]]
        for i in range(2):
            at = slice(3 * i, 3 * i + 3)
            new_up = base[g, at, 0:half, :] + HOPPING * upper[i]
            new_low = base[g, at, half : 2 * half, :] + HOPPING * lower[i]
            field[g, at, 0:half, :] = new_up.astype(bf16).astype(f32)
            field[g, at, half : 2 * half, :] = new_low.astype(bf16).astype(f32)

    loads[1].wait()
    link_wide[...] = link_in[...].astype(f32)
    for mu in range(4):
        for i in range(3):
            for j in range(3):
                for part in range(2):
                    row = ((mu * 3 + i) * 3 + j) * 2 + part
                    links[mu, part, i, j] = jnp.broadcast_to(
                        link_wide[row : row + 1, :], (half, lanes)
                    )

    loads[0].wait()
    wide[...] = src_in[...].astype(f32)

    def arrange(g):
        for pc in range(6):
            for spin in range(4):
                piece = wide[pl.ds((pc * nsrc + g * GROUP) * 4 + spin, GROUP, stride=4), :]
                base[g, pc, spin * GROUP : (spin + 1) * GROUP, :] = piece
                field[g, pc, spin * GROUP : (spin + 1) * GROUP, :] = piece

    loop(groups, arrange)
    pl.semaphore_wait(barrier, peers + 1)

    def spread():
        loads[2].wait()
        elem_all[me] = elem_in[...].astype(elem_all.dtype)
        each(1, peers, lambda off: elem_copy(lax.rem(me + off, peers), me).start())
        loads[3].wait()
        vec_wide[...] = vec_in[...].astype(f32)
        for j in range(6):
            left_mat[0:nmode, j * lanes : (j + 1) * lanes] = vec_wide[
                pl.ds(j, nmode, stride=6), :
            ].astype(bf16)

    def mix():
        def arrive(off):
            p = lax.rem(me + off, peers)
            elem_copy(p, p).wait_recv()

        each(1, peers, arrive)
        for p in range(peers):
            for part in range(2):
                elem_full[part, p * modes_dev : (p + 1) * modes_dev, :] = elem_all[
                    p, part
                ].astype(f32)
        e_re, e_im = elem_full[0].astype(bf16), elem_full[1].astype(bf16)
        blocks = jnp.concatenate(
            [
                jnp.concatenate([e_re, e_im], 1),
                jnp.concatenate([-e_im, e_re], 1),
            ],
            0,
        )
        for c in range(3):
            both = jnp.concatenate(
                [
                    left_mat[0:nmode, (2 * c + part) * lanes : (2 * c + part + 1) * lanes]
                    for part in range(2)
                ],
                0,
            )
            mixed = jnp.dot(blocks, both, preferred_element_type=f32).astype(bf16)
            for part in range(2):
                left_mat[
                    nmode : 2 * nmode, (2 * c + part) * lanes : (2 * c + part + 1) * lanes
                ] = mixed[part * nmode : (part + 1) * nmode]

    def step(sweep):
        def group(g):
            @pl.when(sweep > 0)
            def _():
                finish(sweep - 1, g)

            send_z(sweep, g, True, True)

        loop(groups, group)
        loop(groups, lambda g: send_t(sweep, g, True, True))
        pl.when(sweep == 0)(spread)
        loop(groups, plane)
        pl.when(sweep == 1)(mix)

    loop(SWEEPS, step)

    count = 4 * nsrc
    chunk = 4 * GROUP

    def close(g):
        finish(SWEEPS - 1, g)
        for pc in range(6):
            for spin in range(4):
                wide[pl.ds((g * 6 + pc) * chunk + spin, GROUP, stride=4), :] = field[
                    g, pc, spin * GROUP : (spin + 1) * GROUP, :
                ]
        rows = pl.ds(pl.multiple_of(2 * g * chunk, 2 * chunk), 2 * chunk)
        for c in range(3):
            re_at, im_at = [
                pl.multiple_of((g * 6 + 3 * part + c) * chunk, chunk) for part in range(2)
            ]
            re, im = wide[pl.ds(re_at, chunk), :], wide[pl.ds(im_at, chunk), :]
            at = 2 * c * lanes
            right_mat[rows, at : at + lanes] = jnp.concatenate([re, im], 0).astype(bf16)
            right_mat[rows, at + lanes : at + 2 * lanes] = jnp.concatenate(
                [im, -re], 0
            ).astype(bf16)

    loop(groups, close)
    sums[:, 0 : 2 * count] = lax.dot_general(
        left_mat[...], right_mat[...], (((1,), (1,)), ((), ())), preferred_element_type=f32
    )
    for p in range(peers):
        for o in range(2):
            at = o * nmode + p * modes_dev
            part_out[p, o] = sums[at : at + modes_dev, :].astype(part_out.dtype)
    each(1, peers, lambda off: part_copy(lax.rem(me + off, peers), me).start())

    turned[...] = jnp.zeros_like(turned)
    for o in range(2):
        turned[o * modes_dev : (o + 1) * modes_dev, :] = part_out[me, o].astype(f32)

    def settle(off):
        p = lax.rem(me + off, peers)
        elem_copy(p, me).wait_send()
        part_copy(p, me).wait_send()

    def settle_group(index):
        for way in range(4):
            halo(0, index, way).wait_send()

    loop(SWEEPS * groups, settle_group)
    each(1, peers, settle)

    def gather(off):
        p = lax.rem(me + off, peers)
        part_copy(p, p).wait_recv()
        for o in range(2):
            turned[o * modes_dev : (o + 1) * modes_dev, :] += part_in[p, o].astype(f32)

    each(1, peers, gather)
    flipped = turned[...].T
    for g in range(groups):
        for part in range(2):
            got = flipped[(2 * g + part) * chunk : (2 * g + part + 1) * chunk]
            to = slice(part * count + g * chunk, part * count + (g + 1) * chunk)
            proj_ref[to, :] = got[:, 0:modes_dev]
            cont_ref[to, :] = got[:, modes_dev : 2 * modes_dev]


def local(sources, gauge_links, eigenvectors, elementals):
    slices, peers = lax.axis_size("tm"), lax.axis_size("space")
    _, _, _, _, nsrc, _, lanes = sources.shape
    nmode = eigenvectors.shape[1]
    modes_dev = elementals.shape[2]
    src = sources.transpose(0, 1, 3, 4, 5, 2, 6).reshape(24 * nsrc, lanes)
    link = gauge_links.transpose(0, 1, 3, 4, 5, 2, 6).reshape(72, lanes)
    vec = eigenvectors.transpose(0, 1, 3, 4, 2, 5).reshape(6 * nmode, lanes)
    elem = elementals.reshape(2, modes_dev, nmode)
    groups, half = nsrc // GROUP, 2 * GROUP
    halos = SWEEPS * groups * 4
    src, link, vec, elem = [
        pltpu.with_memory_space_constraint(x, pltpu.HBM) for x in (src, link, vec, elem)
    ]
    kind = bf16 if modes_dev % 16 == 0 else f32
    outs = jax.ShapeDtypeStruct((8 * nsrc, modes_dev), f32)
    dma = pltpu.SemaphoreType.DMA
    vmem = pl.BlockSpec(memory_space=pltpu.VMEM)
    proj, cont = pl.pallas_call(
        functools.partial(kernel, slices, peers, nsrc, modes_dev),
        out_shape=(outs, outs),
        in_specs=[pl.BlockSpec(memory_space=pltpu.HBM)] * 4,
        out_specs=[vmem] * 2,
        scratch_shapes=[
            pltpu.VMEM(src.shape, bf16),
            pltpu.VMEM(link.shape, bf16),
            pltpu.VMEM(vec.shape, bf16),
            pltpu.VMEM(elem.shape, f32),
            dma((4,)),
            pltpu.VMEM(src.shape, f32),
            pltpu.VMEM(link.shape, f32),
            pltpu.VMEM((4, 2, 3, 3, half, lanes), f32),
            pltpu.VMEM((groups, 6, 2 * half, lanes), f32),
            pltpu.VMEM((groups, 6, 2 * half, lanes), f32),
            pltpu.VMEM((groups, 4, 3, half, lanes), f32),
            pltpu.VMEM(vec.shape, f32),
            pltpu.VMEM((halos, 6 * half, lanes), bf16),
            pltpu.VMEM((halos, 6 * half, lanes), bf16),
            dma((halos,)),
            dma((halos,)),
            pltpu.VMEM((peers, 2, modes_dev, nmode), kind),
            pltpu.VMEM((2, nmode, nmode), f32),
            dma((peers,)),
            dma((peers,)),
            pltpu.VMEM((2 * nmode, 6 * lanes), bf16),
            pltpu.VMEM((8 * nsrc, 6 * lanes), bf16),
            pltpu.VMEM((2 * nmode, 128), f32),
            pltpu.VMEM((peers, 2, modes_dev, 128), kind),
            pltpu.VMEM((peers, 2, modes_dev, 128), kind),
            dma((peers,)),
            dma((peers,)),
            pltpu.VMEM((128, 128), f32),
        ],
        compiler_params=pltpu.CompilerParams(
            collective_id=0, has_side_effects=True, vmem_limit_bytes=32 * 1024 * 1024
        ),
        cost_estimate=pl.CostEstimate(
            flops=200_000_000, bytes_accessed=1_000_000, transcendentals=0
        ),
    )(src, link, vec, elem)

    def placed(out):
        return out.reshape(1, 2, nsrc, 4, modes_dev).transpose(0, 1, 3, 2, 4)

    return placed(proj), placed(cont)


def solution(mesh):
    placed = (
        P("tm", None, None, None, None, "space", None),
        P(None, "tm", None, None, None, "space", None),
        P("tm", None, None, None, "space", None),
        P("tm", None, "space", None),
    )
    return jax.shard_map(
        local,
        mesh=mesh,
        in_specs=placed,
        out_specs=(P("tm", None, None, None, "space"), P("tm", None, None, None, "space")),
        check_vma=False,
    )
```

```python
import functools

import jax
import jax.numpy as jnp
from jax import lax
from jax.experimental import pallas as pl
from jax.experimental.pallas import tpu as pltpu
from jax.sharding import PartitionSpec as P

LX = 8
HOPPING = 0.125
SWEEPS = 3
GROUP = 4
MESH = pl.DeviceIdType.MESH
f32 = jnp.float32
bf16 = jnp.bfloat16


def each(lower, upper, body):
    lax.fori_loop(lower, upper, lambda index, carry: (body(index), carry)[1], 0)


def loop(count, body):
    each(0, count, body)


def kernel(
    slices, peers, nsrc, modes_dev,
    src_hbm, link_hbm, vec_hbm, elem_hbm,
    proj_ref, cont_ref,
    src_in, link_in, vec_in, elem_in, load_sem,
    wide, link_wide, links, base, field, hops, vec_wide,
    halo_out, halo_in, halo_send, halo_recv,
    elem_all, elem_full, elem_send, elem_recv,
    left_mat, right_mat, sums, part_out, part_in, part_send, part_recv, turned,
):
    groups = nsrc // GROUP
    half = 2 * GROUP
    lanes = base.shape[-1]
    nmode = peers * modes_dev
    t = lax.axis_index("tm")
    me = lax.axis_index("space")
    t_up, t_down = lax.rem(t + 1, slices), lax.rem(t + slices - 1, slices)
    z_up, z_down = lax.rem(me + 1, peers), lax.rem(me + peers - 1, peers)

    barrier = pltpu.get_barrier_semaphore()

    loads = [
        pltpu.make_async_copy(a, b, load_sem.at[i])
        for i, (a, b) in enumerate(
            ((src_hbm, src_in), (link_hbm, link_in), (elem_hbm, elem_in), (vec_hbm, vec_in))
        )
    ]
    for load in loads:
        load.start()

    def greet(off):
        pl.semaphore_signal(
            barrier, inc=1, device_id=(t, lax.rem(me + off, peers)), device_id_type=MESH
        )

    for near in (t_up, t_down):
        pl.semaphore_signal(barrier, inc=1, device_id=(near, me), device_id_type=MESH)
    each(1, peers, greet)

    row_at = lax.broadcasted_iota(jnp.int32, (1, half, lanes), 1)
    spin_sign = jnp.where(row_at < GROUP, 1.0, -1.0).astype(f32)
    column = lax.broadcasted_iota(jnp.int32, (1, half, lanes), 2) % LX
    ahead_sign = jnp.where(t == slices - 1, -1.0, 1.0).astype(f32)
    behind_sign = jnp.where(t == 0, -1.0, 1.0).astype(f32)

    def apply(mu, pair, dagger):
        re, im = pair
        out_re = out_im = None
        for j in range(3):
            if dagger:
                g_re, g_im = links[mu, 0, j], links[mu, 1, j]
            else:
                g_re, g_im = links[mu, 0, :, j], links[mu, 1, :, j]
            v_re, v_im = re[j][None], im[j][None]
            if dagger:
                add_re, add_im = g_re * v_re + g_im * v_im, g_re * v_im - g_im * v_re
            else:
                add_re, add_im = g_re * v_re - g_im * v_im, g_re * v_im + g_im * v_re
            out_re = add_re if out_re is None else out_re + add_re
            out_im = add_im if out_im is None else out_im + add_im
        return out_re, out_im

    def shift(pair, direction, ahead):
        out = []
        for v in pair:
            if direction == 1:
                out.append(pltpu.roll(v, lanes - LX if ahead else LX, 2))
            else:
                near = pltpu.roll(v, lanes - 1 if ahead else 1, 2)
                wrap = pltpu.roll(v, LX - 1 if ahead else lanes - LX + 1, 2)
                out.append(jnp.where(column == (LX - 1 if ahead else 0), wrap, near))
        return tuple(out)

    def packed(pair):
        return jnp.concatenate([v.reshape(3 * half, lanes) for v in pair], 0).astype(bf16)

    def unpacked(value):
        value = value.astype(f32).reshape(6, half, lanes)
        return value[:3], value[3:]

    def halo(sweep, g, way):
        first = (sweep * 4 + way) * groups
        at = first if way < 2 else first + g
        block = pl.ds(first, groups) if way < 2 else at
        target = ((t_down, me), (t_up, me), (t, z_down), (t, z_up))[way]
        return pltpu.make_async_remote_copy(
            src_ref=halo_out.at[block],
            dst_ref=halo_in.at[block],
            send_sem=halo_send.at[at],
            recv_sem=halo_recv.at[at],
            device_id=target,
            device_id_type=MESH,
        )

    def send(sweep, g, way, pair):
        halo_out[(sweep * 4 + way) * groups + g] = packed(pair)
        if way >= 2:
            halo(sweep, g, way).start()

    def receive(sweep, g, way):
        if way < 2:
            pl.when(g == 0)(lambda: halo(sweep, g, way).wait_recv())
        else:
            halo(sweep, g, way).wait_recv()
        return unpacked(halo_in[(sweep * 4 + way) * groups + g])

    def elem_copy(to, slot):
        return pltpu.make_async_remote_copy(
            src_ref=elem_all.at[me],
            dst_ref=elem_all.at[slot],
            send_sem=elem_send.at[to],
            recv_sem=elem_recv.at[slot],
            device_id=(t, to),
            device_id_type=MESH,
        )

    def part_copy(to, slot):
        return pltpu.make_async_remote_copy(
            src_ref=part_out.at[to],
            dst_ref=part_in.at[slot],
            send_sem=part_send.at[to],
            recv_sem=part_recv.at[slot],
            device_id=(t, to),
            device_id_type=MESH,
        )

    def parts_of(g):
        up = [field[g, 3 * i : 3 * i + 3, 0:half, :] for i in range(2)]
        low = [field[g, 3 * i : 3 * i + 3, half : 2 * half, :] for i in range(2)]
        return up, low

    def turn_z(low):
        return spin_sign * low[1], -(spin_sign * low[0])

    def send_z(sweep, g, minus, plus):
        up, low = parts_of(g)
        turn = turn_z(low)
        if minus:
            send(sweep, g, 2, (up[0] - turn[0], up[1] - turn[1]))
        if plus:
            send(sweep, g, 3, apply(2, (up[0] + turn[0], up[1] + turn[1]), True))

    def send_t(sweep, g, minus, plus):
        up, low = parts_of(g)
        if minus:
            send(sweep, g, 0, (up[0] - low[0], up[1] - low[1]))
        if plus:
            send(sweep, g, 1, apply(3, (up[0] + low[0], up[1] + low[1]), True))

    def plane(g):
        up, low = parts_of(g)
        swapped = [pltpu.roll(v, GROUP, 1) for v in low]
        turned_x = (swapped[1], -swapped[0])
        turned_y = (-(spin_sign * swapped[0]), -(spin_sign * swapped[1]))
        ahead = {}
        behind = {}
        for mu, moved in ((0, turned_x), (1, turned_y)):
            ahead[mu] = apply(
                mu, shift((up[0] - moved[0], up[1] - moved[1]), mu, True), False
            )
            behind[mu] = shift(
                apply(mu, (up[0] + moved[0], up[1] + moved[1]), True), mu, False
            )
        dx = [behind[0][i] - ahead[0][i] for i in range(2)]
        dy = [behind[1][i] - ahead[1][i] for i in range(2)]
        cross = (-dx[1] - spin_sign * dy[0], dx[0] - spin_sign * dy[1])
        for i in range(2):
            hops[g, i] = ahead[0][i] + behind[0][i] + ahead[1][i] + behind[1][i]
            hops[g, 2 + i] = pltpu.roll(cross[i], GROUP, 1)

    def finish(sweep, g):
        f_t = apply(3, receive(sweep, g, 0), False)
        b_t = receive(sweep, g, 1)
        f_t = [ahead_sign * v for v in f_t]
        b_t = [behind_sign * v for v in b_t]
        f_z = apply(2, receive(sweep, g, 2), False)
        b_z = receive(sweep, g, 3)
        dz = [b_z[i] - f_z[i] for i in range(2)]
        upper = [hops[g, i] + f_t[i] + b_t[i] + f_z[i] + b_z[i] for i in range(2)]
        lower = [hops[g, 2 + i] + b_t[i] - f_t[i] for i in range(2)]
        lower = [lower[0] - spin_sign * dz[1], lower[1] + spin_sign * dz[0]]
        for i in range(2):
            at = slice(3 * i, 3 * i + 3)
            new_up = base[g, at, 0:half, :] + HOPPING * upper[i]
            new_low = base[g, at, half : 2 * half, :] + HOPPING * lower[i]
            field[g, at, 0:half, :] = new_up.astype(bf16).astype(f32)
            field[g, at, half : 2 * half, :] = new_low.astype(bf16).astype(f32)

    loads[1].wait()
    link_wide[...] = link_in[...].astype(f32)
    for mu in range(4):
        for i in range(3):
            for j in range(3):
                for part in range(2):
                    row = ((mu * 3 + i) * 3 + j) * 2 + part
                    links[mu, part, i, j] = jnp.broadcast_to(
                        link_wide[row : row + 1, :], (half, lanes)
                    )

    loads[0].wait()
    wide[...] = src_in[...].astype(f32)

    def arrange(g):
        for pc in range(6):
            for spin in range(4):
                piece = wide[pl.ds((pc * nsrc + g * GROUP) * 4 + spin, GROUP, stride=4), :]
                base[g, pc, spin * GROUP : (spin + 1) * GROUP, :] = piece
                field[g, pc, spin * GROUP : (spin + 1) * GROUP, :] = piece

    loop(groups, arrange)
    pl.semaphore_wait(barrier, peers + 1)

    def spread():
        loads[2].wait()
        elem_all[me] = elem_in[...].astype(elem_all.dtype)
        each(1, peers, lambda off: elem_copy(lax.rem(me + off, peers), me).start())
        loads[3].wait()
        vec_wide[...] = vec_in[...].astype(f32)
        for j in range(6):
            left_mat[0:nmode, j * lanes : (j + 1) * lanes] = vec_wide[
                pl.ds(j, nmode, stride=6), :
            ].astype(bf16)

    def mix():
        def arrive(off):
            p = lax.rem(me + off, peers)
            elem_copy(p, p).wait_recv()

        each(1, peers, arrive)
        for p in range(peers):
            for part in range(2):
                elem_full[part, p * modes_dev : (p + 1) * modes_dev, :] = elem_all[
                    p, part
                ].astype(f32)
        e_re, e_im = elem_full[0].astype(bf16), elem_full[1].astype(bf16)
        blocks = jnp.concatenate(
            [
                jnp.concatenate([e_re, e_im], 1),
                jnp.concatenate([-e_im, e_re], 1),
            ],
            0,
        )
        for c in range(3):
            both = jnp.concatenate(
                [
                    left_mat[0:nmode, (2 * c + part) * lanes : (2 * c + part + 1) * lanes]
                    for part in range(2)
                ],
                0,
            )
            mixed = jnp.dot(blocks, both, preferred_element_type=f32).astype(bf16)
            for part in range(2):
                left_mat[
                    nmode : 2 * nmode, (2 * c + part) * lanes : (2 * c + part + 1) * lanes
                ] = mixed[part * nmode : (part + 1) * nmode]

    def step(sweep):
        def group(g):
            @pl.when(sweep > 0)
            def _():
                finish(sweep - 1, g)

            send_z(sweep, g, True, True)

        loop(groups, group)
        for way in range(2):
            loop(groups, lambda g: send_t(sweep, g, way == 0, way == 1))
            halo(sweep, 0, way).start()
        pl.when(sweep == 0)(spread)
        loop(groups, plane)
        pl.when(sweep == 1)(mix)

    loop(SWEEPS, step)

    count = 4 * nsrc
    chunk = 4 * GROUP

    def close(g):
        finish(SWEEPS - 1, g)
        for pc in range(6):
            for spin in range(4):
                wide[pl.ds((g * 6 + pc) * chunk + spin, GROUP, stride=4), :] = field[
                    g, pc, spin * GROUP : (spin + 1) * GROUP, :
                ]
        rows = pl.ds(pl.multiple_of(2 * g * chunk, 2 * chunk), 2 * chunk)
        for c in range(3):
            re_at, im_at = [
                pl.multiple_of((g * 6 + 3 * part + c) * chunk, chunk) for part in range(2)
            ]
            re, im = wide[pl.ds(re_at, chunk), :], wide[pl.ds(im_at, chunk), :]
            at = 2 * c * lanes
            right_mat[rows, at : at + lanes] = jnp.concatenate([re, im], 0).astype(bf16)
            right_mat[rows, at + lanes : at + 2 * lanes] = jnp.concatenate(
                [im, -re], 0
            ).astype(bf16)

    loop(groups, close)
    sums[:, 0 : 2 * count] = lax.dot_general(
        left_mat[...], right_mat[...], (((1,), (1,)), ((), ())), preferred_element_type=f32
    )
    for p in range(peers):
        for o in range(2):
            at = o * nmode + p * modes_dev
            part_out[p, o] = sums[at : at + modes_dev, :].astype(part_out.dtype)
    each(1, peers, lambda off: part_copy(lax.rem(me + off, peers), me).start())

    turned[...] = jnp.zeros_like(turned)
    for o in range(2):
        turned[o * modes_dev : (o + 1) * modes_dev, :] = part_out[me, o].astype(f32)

    def settle(off):
        p = lax.rem(me + off, peers)
        elem_copy(p, me).wait_send()
        part_copy(p, me).wait_send()

    def settle_sweep(sweep):
        for way in range(4):
            each(0, 1 if way < 2 else groups, lambda g: halo(sweep, g, way).wait_send())

    loop(SWEEPS, settle_sweep)
    each(1, peers, settle)

    def gather(off):
        p = lax.rem(me + off, peers)
        part_copy(p, p).wait_recv()
        for o in range(2):
            turned[o * modes_dev : (o + 1) * modes_dev, :] += part_in[p, o].astype(f32)

    each(1, peers, gather)
    flipped = turned[...].T
    for g in range(groups):
        for part in range(2):
            got = flipped[(2 * g + part) * chunk : (2 * g + part + 1) * chunk]
            to = slice(part * count + g * chunk, part * count + (g + 1) * chunk)
            proj_ref[to, :] = got[:, 0:modes_dev]
            cont_ref[to, :] = got[:, modes_dev : 2 * modes_dev]


def local(sources, gauge_links, eigenvectors, elementals):
    slices, peers = lax.axis_size("tm"), lax.axis_size("space")
    _, _, _, _, nsrc, _, lanes = sources.shape
    nmode = eigenvectors.shape[1]
    modes_dev = elementals.shape[2]
    src = sources.transpose(0, 1, 3, 4, 5, 2, 6).reshape(24 * nsrc, lanes)
    link = gauge_links.transpose(0, 1, 3, 4, 5, 2, 6).reshape(72, lanes)
    vec = eigenvectors.transpose(0, 1, 3, 4, 2, 5).reshape(6 * nmode, lanes)
    elem = elementals.reshape(2, modes_dev, nmode)
    groups, half = nsrc // GROUP, 2 * GROUP
    halos = SWEEPS * groups * 4
    src, link, vec, elem = [
        pltpu.with_memory_space_constraint(x, pltpu.HBM) for x in (src, link, vec, elem)
    ]
    kind = bf16 if modes_dev % 16 == 0 else f32
    outs = jax.ShapeDtypeStruct((8 * nsrc, modes_dev), f32)
    dma = pltpu.SemaphoreType.DMA
    vmem = pl.BlockSpec(memory_space=pltpu.VMEM)
    proj, cont = pl.pallas_call(
        functools.partial(kernel, slices, peers, nsrc, modes_dev),
        out_shape=(outs, outs),
        in_specs=[pl.BlockSpec(memory_space=pltpu.HBM)] * 4,
        out_specs=[vmem] * 2,
        scratch_shapes=[
            pltpu.VMEM(src.shape, bf16),
            pltpu.VMEM(link.shape, bf16),
            pltpu.VMEM(vec.shape, bf16),
            pltpu.VMEM(elem.shape, f32),
            dma((4,)),
            pltpu.VMEM(src.shape, f32),
            pltpu.VMEM(link.shape, f32),
            pltpu.VMEM((4, 2, 3, 3, half, lanes), f32),
            pltpu.VMEM((groups, 6, 2 * half, lanes), f32),
            pltpu.VMEM((groups, 6, 2 * half, lanes), f32),
            pltpu.VMEM((groups, 4, 3, half, lanes), f32),
            pltpu.VMEM(vec.shape, f32),
            pltpu.VMEM((halos, 6 * half, lanes), bf16),
            pltpu.VMEM((halos, 6 * half, lanes), bf16),
            dma((halos,)),
            dma((halos,)),
            pltpu.VMEM((peers, 2, modes_dev, nmode), kind),
            pltpu.VMEM((2, nmode, nmode), f32),
            dma((peers,)),
            dma((peers,)),
            pltpu.VMEM((2 * nmode, 6 * lanes), bf16),
            pltpu.VMEM((8 * nsrc, 6 * lanes), bf16),
            pltpu.VMEM((2 * nmode, 128), f32),
            pltpu.VMEM((peers, 2, modes_dev, 128), kind),
            pltpu.VMEM((peers, 2, modes_dev, 128), kind),
            dma((peers,)),
            dma((peers,)),
            pltpu.VMEM((128, 128), f32),
        ],
        compiler_params=pltpu.CompilerParams(
            collective_id=0, has_side_effects=True, vmem_limit_bytes=32 * 1024 * 1024
        ),
        cost_estimate=pl.CostEstimate(
            flops=200_000_000, bytes_accessed=1_000_000, transcendentals=0
        ),
    )(src, link, vec, elem)

    def placed(out):
        return out.reshape(1, 2, nsrc, 4, modes_dev).transpose(0, 1, 3, 2, 4)

    return placed(proj), placed(cont)


def solution(mesh):
    placed = (
        P("tm", None, None, None, None, "space", None),
        P(None, "tm", None, None, None, "space", None),
        P("tm", None, None, None, "space", None),
        P("tm", None, "space", None),
    )
    return jax.shard_map(
        local,
        mesh=mesh,
        in_specs=placed,
        out_specs=(P("tm", None, None, None, "space"), P("tm", None, None, None, "space")),
        check_vma=False,
    )
```
